32 devices in a mesh: grp: 2 (over x), sfc: 16 (over z, y, core).
Axes of the slice: x: 2, y: 2, z: 4, core: 2. Of those that a mesh axis runs over, the one named last changes fastest.
Arguments:
- tracers: float32 [8, 64, 16384], P(None, None, ('grp', 'sfc')), parts along dimension 2, may hold values from -6 to 6
- velocity: float32 [2, 64, 16384], P(None, None, ('grp', 'sfc')), parts along dimension 2, may hold values from -4 to 4
- metric: float32 [16384], P(('grp', 'sfc')), parts along dimension 0, may hold values from 0.5 to 2
- absorber: bfloat16 [16384, 256], P(('grp', 'sfc')), parts along dimension 0, may hold values from 0.049804688 to 1
- cosine_zenith: bfloat16 [16384], P(('grp', 'sfc')), parts along dimension 0, may hold values from 0.049804688 to 1
- layer_mass: bfloat16 [64, 16384], P(None, ('grp', 'sfc')), parts along dimension 1, may hold values from 0.5 to 2
- absorption: bfloat16 [4, 112, 64], replicated, may hold values from 0.0009994507 to 0.29882812
- solar_flux: float32 [112], replicated, may hold values from 0.1 to 1
- sunlit: int32 [128], P(('grp', 'sfc')), parts along dimension 0, may hold values from 0 to 1, as said below
- neighbour: int32 [4, 1024], P(None, ('grp', 'sfc')), parts along dimension 1, may hold values from 0 to 511, as said below
- neighbour_edge: int32 [4, 1024], P(None, ('grp', 'sfc')), parts along dimension 1, may hold values from 0 to 3
Outputs:
- advanced: float32 [8, 64, 16384], P(None, None, ('grp', 'sfc')), parts along dimension 2
- heating: float32 [64, 16384], P(None, ('grp', 'sfc')), parts along dimension 1
The draws below stay inside these ranges and needn't reach their ends.
There are 2 independent parts, one for each index of `grp`. The reference program is written for one: setup_inputs(seed, part) draws one part's arguments, and reference() takes and returns one part's arrays. A program takes and returns all parts, laid end to end along the dimension named above; an argument that names none is the same for every part. Nothing has to cross between parts.
Inputs may be any that keep to these rules, and one draw needn't show every extreme that they name: `sunlit`: the 1s form one cyclic run of 32 consecutive blocks; all other blocks are 0. For an element among the 32 elements of device position d along sfc (elements d * 32 to (d + 1) * 32 - 1), every neighbour lies among those elements or the 8 elements on either side of them, counted cyclically over 512; on every device both ends of that range are named.
All inputs are finite; a program needn't handle non-finite values.
Results may differ from the reference program's by a relative error of at most 0.0003.
Values may be sent and summed in bfloat16 or wider, within the bound.
No kernel may reach another device: no remote copies, remote signals or barrier semaphores. Data moves between devices by JAX's collectives and lax.ppermute only.
A program may use at most 64 MiB of HBM per device.

```python
import math
import jax
import jax.numpy as jnp
import numpy as np
from jax import lax

TRACERS = 8
LEVELS = 64
GPOINTS = 112
GASES = 4
BLOCK_COLS = 128
RIM = 8
E_DEV = 32
ELEMS = 512
COLS = 8192
BLOCKS = 64


def draw_sunlit(key, part):
    key = jax.random.fold_in(key, 5)
    start_block = jax.random.randint(key, (), 0, BLOCKS)
    block_ids = jnp.arange(BLOCKS, dtype=jnp.int32)
    return ((block_ids - start_block) % BLOCKS < BLOCKS // 2).astype(jnp.int32)


def draw_neighbour(key, part):
    key = jax.random.fold_in(key, 11)
    element = jnp.arange(ELEMS, dtype=jnp.int32)
    device = element // E_DEV
    lowest = device * E_DEV - RIM
    offset = jax.random.randint(key, (4, ELEMS), 0, E_DEV + 2 * RIM)
    picked = (lowest[None, :] + offset) % ELEMS
    first_of = element % E_DEV == 0
    last_of = element % E_DEV == E_DEV - 1
    edge_one = jnp.where(first_of, (device * E_DEV - RIM) % ELEMS, jnp.where(last_of, ((device + 1) * E_DEV + RIM - 1) % ELEMS, picked[1]))
    picked = picked.at[1].set(edge_one)
    edge_three = jnp.where(element == 0, ELEMS - 1, jnp.where(element == ELEMS - 1, 0, picked[3]))
    picked = picked.at[3].set(edge_three)
    return picked.astype(jnp.int32)


def touch_ends(entries, own_key, smallest, largest):
    shape = entries.shape
    spot = [jax.random.randint(jax.random.fold_in(own_key, axis), (), 0, shape[axis]) for axis in range(len(shape))]
    entries = entries.at[tuple(spot)].set(smallest)
    longest = shape.index(max(shape))
    spot[longest] = (spot[longest] + 1) % shape[longest]
    return entries.at[tuple(spot)].set(largest)


def block_levels(stream_key, dims, cuts, smallest, top_value):
    loudness, own = 1.0, jax.random.fold_in(stream_key, 6)
    for position, parts in cuts:
        steps = jnp.exp(jax.random.uniform(jax.random.fold_in(own, position), (parts,), jnp.float32, smallest / len(cuts), top_value / len(cuts)))
        loudness = loudness * jnp.repeat(steps, dims[position] // parts).reshape([-1 if axis == position else 1 for axis in range(len(dims))])
    return loudness


def scatter_about(key, extent, deviation, limit, shards=(), kind=jnp.bfloat16):
    level = block_levels(key, extent, shards, -0.22, 0.18) if shards else 1.0
    drawn = jax.random.normal(key, extent, jnp.float32) * deviation * level
    return jnp.minimum(jnp.maximum(drawn, -limit), limit).astype(kind)


def setup_inputs(seed: int = 0, part: int = 0) -> dict:
    key_of = jax.random.split(jax.random.key(seed), 12)
    part_keys = jax.random.split(jax.random.fold_in(key_of[11], part), 12)
    return {
        "tracers": scatter_about(part_keys[0], (TRACERS, LEVELS, COLS), 1.0, 6.0, ((2, 16),), jnp.float32),
        "velocity": scatter_about(part_keys[1], (2, LEVELS, COLS), 1.0, 4.0, ((2, 16),), jnp.float32),
        "metric": jnp.clip(jnp.exp(math.log(2.0) - 1.3862944 * jax.random.uniform(part_keys[2], (COLS,), jnp.float32) ** block_levels(part_keys[2], (COLS,), ((0, 16),), -0.2, 0.2)), 0.5, 2.0),
        "absorber": jnp.clip(jnp.exp(math.log(1.0) - 2.9996462 * jax.random.uniform(part_keys[3], (COLS, GASES * LEVELS), jnp.float32) ** block_levels(part_keys[3], (COLS, GASES * LEVELS), ((0, 16),), -0.2, 0.2)), 0.049804688, 1.0).astype(jnp.bfloat16),
        "cosine_zenith": jnp.clip(0.049804688 + 0.9501953 * jax.random.uniform(part_keys[4], (COLS,), jnp.float32) ** block_levels(part_keys[4], (COLS,), ((0, 16),), -0.2, 0.2), 0.049804688, 1.0).astype(jnp.bfloat16),
        "layer_mass": jnp.clip(jnp.exp(math.log(2.0) - 1.3862944 * jax.random.uniform(part_keys[5], (LEVELS, COLS), jnp.float32) ** block_levels(part_keys[5], (LEVELS, COLS), ((1, 16),), -0.2, 0.2)), 0.5, 2.0).astype(jnp.bfloat16),
        "absorption": jnp.clip(jnp.exp(jax.random.uniform(key_of[6], (GASES, GPOINTS, LEVELS), jnp.float32, math.log(0.0009994507), math.log(0.29882812))), 0.0009994507, 0.29882812).astype(jnp.bfloat16),
        "solar_flux": jnp.clip(jnp.exp(jax.random.uniform(key_of[7], (GPOINTS,), jnp.float32, math.log(0.1), math.log(1.0))), 0.1, 1.0),
        "sunlit": draw_sunlit(jax.random.fold_in(jax.random.fold_in(key_of[11], part), 71), part),
        "neighbour": draw_neighbour(jax.random.fold_in(jax.random.fold_in(key_of[11], part), 71), part),
        "neighbour_edge": touch_ends(jax.random.randint(part_keys[10], (4, ELEMS), 0, 4), jax.random.fold_in(part_keys[10], 1), 0, 3).astype(jnp.int32),
    }


time_step = 0.1

def derivative_table():
    gll_nodes = np.array([-1.0, -1.0 / math.sqrt(5.0), 1.0 / math.sqrt(5.0), 1.0])
    bary_weights = np.array([1.0 / np.prod([gll_nodes[ipoint] - gll_nodes[mpoint] for mpoint in range(4) if mpoint != ipoint]) for ipoint in range(4)])
    deriv_table = np.zeros((4, 4))
    for ipoint in range(4):
        for mpoint in range(4):
            if ipoint != mpoint:
                deriv_table[ipoint, mpoint] = bary_weights[mpoint] / bary_weights[ipoint] / (gll_nodes[ipoint] - gll_nodes[mpoint])
        deriv_table[ipoint, ipoint] = -sum((deriv_table[ipoint, mpoint] for mpoint in range(4) if mpoint != ipoint))
    return deriv_table

def as_points(field):
    return field.reshape(field.shape[:-1] + (-1, 4, 4))

def tendency(state_field, velocity, metric, deriv_table):
    first_axis = jnp.stack([sum((float(deriv_table[ipoint, mpoint]) * state_field[:, :, :, mpoint, :] for mpoint in range(4))) for ipoint in range(4)], axis=3)
    second_axis = jnp.stack([sum((float(deriv_table[jpoint, mpoint]) * state_field[:, :, :, :, mpoint] for mpoint in range(4))) for jpoint in range(4)], axis=4)
    return -(velocity[0] * first_axis + velocity[1] * second_axis) * metric

def edge_values(state_field):
    return jnp.stack([state_field[:, :, :, 0, :], state_field[:, :, :, :, 3], state_field[:, :, :, 3, ::-1], state_field[:, :, :, ::-1, 0]], axis=3)

def apply_edges(state_field, change):
    state_field = state_field.at[:, :, :, 0, :].add(change[:, :, :, 0, :])
    state_field = state_field.at[:, :, :, :, 3].add(change[:, :, :, 1, :])
    state_field = state_field.at[:, :, :, 3, :].add(change[:, :, :, 2, ::-1])
    state_field = state_field.at[:, :, :, :, 0].add(change[:, :, :, 3, ::-1])
    return state_field

def stiffness(state_field, neighbour, neighbour_edge):
    edge_vals = edge_values(state_field)
    elements = state_field.shape[2]
    flattened = edge_vals[:, :, :, :, ::-1].reshape(state_field.shape[0], state_field.shape[1], 4 * elements, 4)
    facing_index = (neighbour * 4 + neighbour_edge).T.reshape(-1).astype(jnp.int32)
    facing = jnp.take(flattened, facing_index, axis=2).reshape(edge_vals.shape)
    return apply_edges(state_field, 0.5 * (facing - edge_vals))

def reference(tracers, velocity, metric, absorber, cosine_zenith, layer_mass, absorption, solar_flux, sunlit, neighbour, neighbour_edge):
    deriv_table = derivative_table()
    tracer_pts = as_points(tracers)
    wind_pts = as_points(velocity)
    metric_pts = as_points(metric)
    first_section = stiffness(tracer_pts + time_step * tendency(tracer_pts, wind_pts, metric_pts, deriv_table), neighbour, neighbour_edge)
    gas_table = absorption.astype(jnp.float32)
    levels = layer_mass.shape[0]
    blocks = sunlit.shape[0]

    def block_heating(pieces):
        amounts, cosines, masses, lit_flag = pieces
        amounts = amounts.astype(jnp.float32).reshape(amounts.shape[0], gas_table.shape[0], levels)
        layer_depth = jnp.einsum('csl,sgl->cgl', amounts, gas_table, precision=lax.Precision.HIGHEST)
        optical_path = jnp.cumsum(layer_depth, axis=2)
        slant_cos = cosines.astype(jnp.float32)
        transmit = jnp.exp(-optical_path / slant_cos[:, None, None])
        downward = jnp.einsum('cgl,g->cl', transmit, solar_flux, precision=lax.Precision.HIGHEST)
        flux_above = jnp.concatenate([jnp.broadcast_to(jnp.sum(solar_flux), (downward.shape[0], 1)), downward[:, :-1]], axis=1)
        return lit_flag * (slant_cos[:, None] * (flux_above - downward)).T / masses.astype(jnp.float32)
    heat_blocks = lax.map(block_heating, (absorber.reshape(blocks, BLOCK_COLS, -1), cosine_zenith.reshape(blocks, BLOCK_COLS), layer_mass.reshape(levels, blocks, BLOCK_COLS).transpose(1, 0, 2), sunlit.astype(jnp.float32)))
    heating = heat_blocks.transpose(1, 0, 2).reshape(levels, -1)
    forcing = as_points(heating)
    section_tendency = tendency(first_section, wind_pts, metric_pts, deriv_table).at[0].add(forcing)
    advanced = stiffness(0.5 * tracer_pts + 0.5 * (first_section + time_step * section_tendency), neighbour, neighbour_edge)
    return (advanced.reshape(tracers.shape), heating)
```

```python
import functools
import math

import jax
import jax.numpy as jnp
import numpy as np
from jax import lax
from jax.experimental import pallas as pl
from jax.experimental.pallas import tpu as pltpu
from jax.sharding import PartitionSpec as P

BLOCK = 128
RIM = 8
STEP = 0.1
F32 = jnp.float32
BF16 = jnp.bfloat16
VMEM = pl.BlockSpec(memory_space=pltpu.VMEM)
SMEM = pl.BlockSpec(memory_space=pltpu.SMEM)
HBM = pl.BlockSpec(memory_space=pl.ANY)


def derivative_table():
    nodes = np.array([-1.0, -1.0 / math.sqrt(5.0), 1.0 / math.sqrt(5.0), 1.0])
    weights = np.array(
        [1.0 / np.prod([nodes[i] - nodes[m] for m in range(4) if m != i]) for i in range(4)]
    )
    table = np.zeros((4, 4))
    for i in range(4):
        for m in range(4):
            if i != m:
                table[i, m] = weights[m] / weights[i] / (nodes[i] - nodes[m])
        table[i, i] = -sum(table[i, m] for m in range(4) if m != i)
    return table


def params(mib=8):
    return pltpu.CompilerParams(vmem_limit_bytes=mib << 20)


def cost(flops, size=1 << 20):
    return pl.CostEstimate(flops=int(flops), bytes_accessed=int(size), transcendentals=0)


def iota(shape, dim):
    return lax.broadcasted_iota(jnp.int32, shape, dim)


def split(x):
    high = x.astype(BF16)
    return high, (x - high.astype(F32)).astype(BF16)


def dot(a, b):
    return jnp.dot(a, b, preferred_element_type=F32)


def build_derivatives(wide_ref, fine_ref):
    table = derivative_table()
    src, dst = iota((BLOCK, BLOCK), 0), iota((BLOCK, BLOCK), 1)
    si, sj, di, dj = src // 4 % 4, src % 4, dst // 4 % 4, dst % 4
    same = src // 16 == dst // 16
    halves = []
    for d, s, keep in ((di, si, same & (sj == dj)), (dj, sj, same & (si == di))):
        pick = jnp.where(keep, d * 4 + s, -1)
        value = jnp.zeros((BLOCK, BLOCK), F32)
        for i in range(4):
            for m in range(4):
                value = jnp.where(pick == i * 4 + m, float(table[i, m]), value)
        halves.append(value)
    high, low = split(jnp.concatenate(halves, axis=1))
    wide_ref[:BLOCK] = high
    wide_ref[BLOCK:] = high
    fine_ref[...] = low


def advance(field, first, second, wide_ref, fine_ref):
    high, low = split(field)
    both = dot(jnp.concatenate([high, low], axis=1), wide_ref[...]) + dot(high, fine_ref[...])
    return field + first * both[:, :BLOCK] + second * both[:, BLOCK:]


def repeat_rows(x, times):
    return jnp.concatenate([x] * times, axis=0) if times > 1 else x


def rim_kernel(levels, tr_hbm, vel_hbm, metric, left, right, wide, fine, tr, vel, sems):
    cols = metric.shape[1]
    starts = (0, cols - BLOCK)
    copies = []
    for r, c0 in enumerate(starts):
        copies.append(pltpu.make_async_copy(vel_hbm.at[:, pl.ds(c0, BLOCK)], vel.at[r], sems.at[r]))
        copies.append(pltpu.make_async_copy(tr_hbm.at[:, pl.ds(c0, BLOCK)], tr.at[r], sems.at[2 + r]))
    for copy in copies:
        copy.start()
    build_derivatives(wide, fine)
    for copy in copies:
        copy.wait()
    rows = tr.shape[1]
    for r, out in enumerate((left, right)):
        scale = -STEP * metric[:, pl.ds(starts[r], BLOCK)]
        first = repeat_rows(vel[r, :levels] * scale, rows // levels)
        second = repeat_rows(vel[r, levels:] * scale, rows // levels)
        out[...] = advance(tr[r], first, second, wide, fine)


def build_assembly(total, position, nb, ne, local, halo):
    elems, cols = nb.shape[1], local.shape[1]
    index = nb[...] - position * elems + RIM
    index = jnp.where(index < 0, index + total, index)
    index = jnp.where(index >= total, index - total, index)
    code = (index * 4 + ne[...]).astype(F32).astype(BF16)
    spread = (iota((elems, cols), 1) // 16 == iota((elems, cols), 0)).astype(F32).astype(BF16)
    code = dot(code, spread).astype(jnp.int32)
    lane = iota((1, cols), 1)
    i, j = lane // 4 % 4, lane % 4

    def source(code, p):
        edge, q = code % 4, 3 - p
        si = jnp.where(edge == 0, 0, jnp.where(edge == 1, q, jnp.where(edge == 2, 3, 3 - q)))
        sj = jnp.where(edge == 0, q, jnp.where(edge == 1, 3, jnp.where(edge == 2, 3 - q, 0)))
        return code // 4 * 16 + si * 4 + sj

    across = jnp.where(i == 0, source(code[0:1], j), source(code[2:3], 3 - j))
    across = jnp.where((i == 0) | (i == 3), across, -1)
    along = jnp.where(j == 3, source(code[1:2], i), source(code[3:4], 3 - i))
    along = jnp.where((j == 0) | (j == 3), along, -1)
    own = 1.0 - 0.5 * ((across >= 0).astype(F32) + (along >= 0).astype(F32))

    def rows_of(start):
        row = iota((BLOCK, cols), 0) + start
        return jnp.where(row == across, 0.5, 0.0) + jnp.where(row == along, 0.5, 0.0)

    halo[:BLOCK] = rows_of(0).astype(BF16)
    halo[BLOCK:] = rows_of(BLOCK + cols).astype(BF16)
    for r in range(0, cols, BLOCK):
        value = rows_of(BLOCK + r) + jnp.where(iota((BLOCK, cols), 0) + r == lane, own, 0.0)
        local[r : r + BLOCK] = value.astype(BF16)


def first_kernel(
    total, levels, chunk, tr, vel, metric, wide, fine, left, right, nb, ne, part, speed, local, halo
):
    rows, cols = tr.shape
    scale = -STEP * metric[...]
    speed[...] = vel[...] * scale
    build_assembly(total, lax.axis_index("sfc"), nb, ne, local, halo)

    def body(c, carry):
        r = pl.ds(pl.multiple_of(c * chunk, chunk), chunk)
        tiles = [left[r]]
        for b in range(BLOCK, cols - BLOCK, BLOCK):
            first = repeat_rows(speed[:levels, b : b + BLOCK], chunk // levels)
            second = repeat_rows(speed[levels:, b : b + BLOCK], chunk // levels)
            tiles.append(advance(tr[r, b : b + BLOCK], first, second, wide, fine))
        tiles.append(right[r])
        high, low = split(jnp.concatenate(tiles, axis=1))
        part[r] = dot(high, local[...]) + dot(low, local[...])
        return carry

    lax.fori_loop(0, rows // chunk, body, 0)


def halo_parts(left, right):
    lh, ll = split(left)
    rh, rl = split(right)
    return jnp.concatenate([lh, rh], axis=1), jnp.concatenate([ll, rl], axis=1)


def rim2_kernel(levels, part, left, right, halo, wide, fine, tr, speed, heat, out_left, out_right):
    rows, cols = part.shape
    high, low = halo_parts(left[...], right[...])
    for r, (c0, out) in enumerate(((0, out_left), (cols - BLOCK, out_right))):
        tile = pl.ds(c0, BLOCK)
        section = part[:, tile] + dot(high, halo[:, tile]) + dot(low, halo[:, tile])
        first = repeat_rows(speed[:levels, tile], rows // levels)
        second = repeat_rows(speed[levels:, tile], rows // levels)
        out[...] = 0.5 * (tr[:, tile] + advance(section, first, second, wide, fine))
        out[:levels] += (0.5 * STEP) * heat[:, r * BLOCK : (r + 1) * BLOCK]


def inner2_kernel(
    levels, chunk, part, left, right, halo, local, wide, fine, tr, speed, heat_rim, heat_in,
    own_left, own_right, out, heating,
):
    rows, cols = part.shape
    heating[:, :BLOCK] = heat_rim[:, :BLOCK]
    heating[:, BLOCK : cols - BLOCK] = heat_in[...]
    heating[:, cols - BLOCK :] = heat_rim[:, BLOCK:]

    def body(c, carry):
        r = pl.ds(pl.multiple_of(c * chunk, chunk), chunk)
        high, low = halo_parts(left[r], right[r])
        inner = halo[:, BLOCK : cols - BLOCK]
        section = part[r, BLOCK : cols - BLOCK] + dot(high, inner) + dot(low, inner)
        tiles = [own_left[r]]
        warm = jnp.where(c == 0, 0.5 * STEP, 0.0)
        for b in range(BLOCK, cols - BLOCK, BLOCK):
            first = repeat_rows(speed[:levels, b : b + BLOCK], chunk // levels)
            second = repeat_rows(speed[levels:, b : b + BLOCK], chunk // levels)
            field = advance(section[:, b - BLOCK : b], first, second, wide, fine)
            field = 0.5 * (tr[r, b : b + BLOCK] + field)
            add = warm * heat_in[:, b - BLOCK : b]
            if chunk > levels:
                add = jnp.concatenate([add, jnp.zeros((chunk - levels, BLOCK), F32)], axis=0)
            tiles.append(field + add)
        tiles.append(own_right[r])
        high, low = split(jnp.concatenate(tiles, axis=1))
        out[r] = dot(high, local[...]) + dot(low, local[...])
        return carry

    lax.fori_loop(0, rows // chunk, body, 0)


def last_kernel(chunk, part, left, right, halo, out):
    def body(c, carry):
        r = pl.ds(pl.multiple_of(c * chunk, chunk), chunk)
        high, low = halo_parts(left[r], right[r])
        out[r] = part[r] + dot(high, halo[...]) + dot(low, halo[...])
        return carry

    lax.fori_loop(0, part.shape[0] // chunk, body, 0)


def heat_kernel(
    blocks, group, absorber, cosine, mass, absorption, flux, lit, out, table, depth
):
    gases, points, levels = absorption.shape
    width = len(blocks) * BLOCK
    any_lit = lit[blocks[0]]
    for b in blocks[1:]:
        any_lit = any_lit + lit[b]

    @pl.when(any_lit == 0)
    def _():
        out[...] = jnp.zeros_like(out)

    @pl.when(any_lit > 0)
    def _():
        table[...] = jnp.concatenate([absorption[s].astype(F32) for s in range(gases)], axis=1)
        amounts = jnp.concatenate([absorber[b * BLOCK : (b + 1) * BLOCK] for b in blocks], axis=0)
        cos = jnp.concatenate([cosine[:, b * BLOCK : (b + 1) * BLOCK] for b in blocks], axis=1)
        cos = cos.astype(F32)
        scale = -math.log2(math.e) / cos
        shape = (levels, gases * levels)
        keep = iota(shape, 1) % levels <= iota(shape, 0)

        def body(c, carry):
            down, top = carry
            rows = []
            for k in range(group):
                row = table[pl.ds(c * group + k, 1), :]
                rows.append(jnp.where(keep, row, 0.0).astype(BF16))
            weights = jnp.concatenate(rows, axis=0)
            depth[...] = lax.dot_general(
                weights, amounts, (((1,), (1,)), ((), ())), preferred_element_type=F32
            )
            for k in range(group):
                f = flux[c * group + k]
                down = down + f * jnp.exp2(depth[k * levels : (k + 1) * levels] * scale)
                top = top + f
            return down, top

        down, top = lax.fori_loop(
            0, points // group, body, (jnp.zeros((levels, width), F32), jnp.float32(0.0))
        )
        above = jnp.concatenate([jnp.full((1, width), top, F32), down[:-1]], axis=0)
        value = cos * (above - down)
        for k, b in enumerate(blocks):
            tile = slice(k * BLOCK, (k + 1) * BLOCK)
            on = jnp.where(lit[b] > 0, 1.0, 0.0)
            weight = mass[:, b * BLOCK : (b + 1) * BLOCK].astype(F32)
            out[:, tile] = on * value[:, tile] / weight


def struct(shape, dtype=F32):
    return jax.ShapeDtypeStruct(shape, dtype)


def shards(
    tracers, velocity, metric, absorber, cosine, mass, absorption, flux, lit, neighbour, edge
):
    count, levels, cols = tracers.shape
    gases, points, _ = absorption.shape
    peers = lax.axis_size("sfc")
    total = neighbour.shape[1] * peers
    rows = count * levels
    up = [(i, (i + 1) % peers) for i in range(peers)]
    down = [(j, i) for i, j in up]
    tr = tracers.reshape(rows, cols)
    vel = velocity.reshape(2 * levels, cols)
    metric = metric.reshape(1, cols)
    cosine = cosine.reshape(1, cols)
    chunk = 2 * levels
    side = struct((rows, BLOCK))

    left, right, wide, fine = pl.pallas_call(
        functools.partial(rim_kernel, levels),
        in_specs=[HBM, HBM, VMEM],
        out_specs=[VMEM] * 4,
        out_shape=[side, side, struct((2 * BLOCK, 2 * BLOCK), BF16), struct((BLOCK, 2 * BLOCK), BF16)],
        scratch_shapes=[
            pltpu.VMEM((2, rows, BLOCK), F32),
            pltpu.VMEM((2, 2 * levels, BLOCK), F32),
            pltpu.SemaphoreType.DMA((4,)),
        ],
        compiler_params=params(),
        name="rims_first",
    )(tr, vel, metric)
    from_left = lax.ppermute(right, "sfc", up)
    from_right = lax.ppermute(left, "sfc", down)

    def heat(blocks, name):
        group = 8
        return pl.pallas_call(
            functools.partial(heat_kernel, blocks, group),
            in_specs=[VMEM] * 4 + [SMEM, SMEM],
            out_specs=VMEM,
            out_shape=struct((levels, len(blocks) * BLOCK)),
            scratch_shapes=[
                pltpu.VMEM((points, gases * levels), F32),
                pltpu.VMEM((group * levels, len(blocks) * BLOCK), F32),
            ],
            compiler_params=params(),
            cost_estimate=cost(1e9),
            name=name,
        )(absorber, cosine, mass, absorption, flux, lit)

    part, speed, local, halo = pl.pallas_call(
        functools.partial(first_kernel, total, levels, chunk),
        in_specs=[VMEM] * 9,
        out_specs=[VMEM] * 4,
        out_shape=[
            struct((rows, cols)),
            struct((2 * levels, cols)),
            struct((cols, cols), BF16),
            struct((2 * BLOCK, cols), BF16),
        ],
        compiler_params=params(),
        cost_estimate=cost(1e9),
        name="first_local",
    )(tr, vel, metric, wide, fine, left, right, neighbour, edge)
    heat_rim = heat((0, 3), "heat_rims")

    own_left, own_right = pl.pallas_call(
        functools.partial(rim2_kernel, levels),
        in_specs=[VMEM] * 9,
        out_specs=[VMEM] * 2,
        out_shape=[side, side],
        compiler_params=params(),
        name="rims_second",
    )(part, from_left, from_right, halo, wide, fine, tr, speed, heat_rim)
    next_left = lax.ppermute(own_right, "sfc", up)
    next_right = lax.ppermute(own_left, "sfc", down)
    heat_in = heat((1, 2), "heat_inner")
    part2, heating = pl.pallas_call(
        functools.partial(inner2_kernel, levels, chunk),
        in_specs=[VMEM] * 13,
        out_specs=[VMEM] * 2,
        out_shape=[struct((rows, cols)), struct((levels, cols))],
        compiler_params=params(),
        cost_estimate=cost(1e9),
        name="second_local",
    )(
        part, from_left, from_right, halo, local, wide, fine, tr, speed, heat_rim, heat_in,
        own_left, own_right,
    )
    advanced = pl.pallas_call(
        functools.partial(last_kernel, chunk),
        in_specs=[VMEM] * 4,
        out_specs=VMEM,
        out_shape=struct((rows, cols)),
        compiler_params=params(),
        name="last",
    )(part2, next_left, next_right, halo)
    return advanced.reshape(tracers.shape), heating


def solution(mesh):
    placed = (
        P(None, None, ("grp", "sfc")),
        P(None, None, ("grp", "sfc")),
        P(("grp", "sfc")),
        P(("grp", "sfc"), None),
        P(("grp", "sfc")),
        P(None, ("grp", "sfc")),
        P(),
        P(),
        P(("grp", "sfc")),
        P(None, ("grp", "sfc")),
        P(None, ("grp", "sfc")),
    )
    return jax.shard_map(
        shards,
        mesh=mesh,
        in_specs=placed,
        out_specs=(P(None, None, ("grp", "sfc")), P(None, ("grp", "sfc"))),
        check_vma=False,
    )
```

```python
import functools
import math

import jax
import jax.numpy as jnp
import numpy as np
from jax import lax
from jax.experimental import pallas as pl
from jax.experimental.pallas import tpu as pltpu
from jax.sharding import PartitionSpec as P

BLOCK = 128
RIM = 8
STEP = 0.1
F32 = jnp.float32
BF16 = jnp.bfloat16
VMEM = pl.BlockSpec(memory_space=pltpu.VMEM)
SMEM = pl.BlockSpec(memory_space=pltpu.SMEM)
HBM = pl.BlockSpec(memory_space=pltpu.HBM)


def derivative_table():
    nodes = np.array([-1.0, -1.0 / math.sqrt(5.0), 1.0 / math.sqrt(5.0), 1.0])
    weights = np.array(
        [1.0 / np.prod([nodes[i] - nodes[m] for m in range(4) if m != i]) for i in range(4)]
    )
    table = np.zeros((4, 4))
    for i in range(4):
        for m in range(4):
            if i != m:
                table[i, m] = weights[m] / weights[i] / (nodes[i] - nodes[m])
        table[i, i] = -sum(table[i, m] for m in range(4) if m != i)
    return table


def params(mib=8):
    return pltpu.CompilerParams(vmem_limit_bytes=mib << 20)


def cost(flops, size=1 << 20):
    return pl.CostEstimate(flops=int(flops), bytes_accessed=int(size), transcendentals=0)


def iota(shape, dim):
    return lax.broadcasted_iota(jnp.int32, shape, dim)


def split(x):
    high = x.astype(BF16)
    return high, (x - high.astype(F32)).astype(BF16)


def dot(a, b):
    return jnp.dot(a, b, preferred_element_type=F32)


def build_derivatives(wide_ref, fine_ref):
    table = derivative_table()
    src, dst = iota((BLOCK, BLOCK), 0), iota((BLOCK, BLOCK), 1)
    si, sj, di, dj = src // 4 % 4, src % 4, dst // 4 % 4, dst % 4
    same = src // 16 == dst // 16
    halves = []
    for d, s, keep in ((di, si, same & (sj == dj)), (dj, sj, same & (si == di))):
        pick = jnp.where(keep, d * 4 + s, -1)
        value = jnp.zeros((BLOCK, BLOCK), F32)
        for i in range(4):
            for m in range(4):
                value = jnp.where(pick == i * 4 + m, float(table[i, m]), value)
        halves.append(value)
    high, low = split(jnp.concatenate(halves, axis=1))
    wide_ref[:BLOCK] = high
    wide_ref[BLOCK:] = high
    fine_ref[...] = low


def advance(field, first, second, wide_ref, fine_ref):
    high, low = split(field)
    both = dot(jnp.concatenate([high, low], axis=1), wide_ref[...]) + dot(high, fine_ref[...])
    return field + first * both[:, :BLOCK] + second * both[:, BLOCK:]


def repeat_rows(x, times):
    return jnp.concatenate([x] * times, axis=0) if times > 1 else x


def rim_starts(cols):
    near = jnp.where(lax.axis_index("sfc") % 2 == 0, cols - BLOCK, 0)
    return pl.multiple_of(near, BLOCK), pl.multiple_of(cols - BLOCK - near, BLOCK)


def rim_kernel(levels, *refs):
    count = (len(refs) - 5) // 2
    given, (near, far, wide, fine), kept, sems = (
        refs[:count], refs[count : count + 4], refs[count + 4 : -1], refs[-1],
    )
    tr_hbm, vel_hbm, metric_hbm = given[:3]
    tr, vel, metric = kept[:3]
    rows, cols = tr.shape
    rims = (pl.ds(0, BLOCK), pl.ds(cols - BLOCK, BLOCK))
    inner = pl.ds(BLOCK, cols - 2 * BLOCK)
    pairs = [(metric_hbm, metric)]
    pairs += [(hbm.at[:, r], ref.at[:, r]) for r in rims for hbm, ref in ((vel_hbm, vel), (tr_hbm, tr))]
    pairs += [(hbm.at[:, inner], ref.at[:, inner]) for hbm, ref in ((vel_hbm, vel), (tr_hbm, tr))]
    pairs += list(zip(given[3:], kept[3:], strict=True))
    copies = [pltpu.make_async_copy(a, b, sems.at[k]) for k, (a, b) in enumerate(pairs)]
    for copy in copies:
        copy.start()
    build_derivatives(wide, fine)
    copies[0].wait()
    for copy in copies[1:5]:
        copy.wait()
    for start, out in zip(rim_starts(cols), (near, far), strict=True):
        rim = pl.ds(start, BLOCK)
        scale = -STEP * metric[:, rim]
        first = repeat_rows(vel[:levels, rim] * scale, rows // levels)
        second = repeat_rows(vel[levels:, rim] * scale, rows // levels)
        out[...] = advance(tr[:, rim], first, second, wide, fine)
    for copy in copies[5:]:
        copy.wait()


def build_assembly(total, position, nb, ne, local, halo):
    elems, cols = nb.shape[1], local.shape[1]
    index = nb[...] - position * elems + RIM
    index = jnp.where(index < 0, index + total, index)
    index = jnp.where(index >= total, index - total, index)
    code = (index * 4 + ne[...]).astype(F32).astype(BF16)
    spread = (iota((elems, cols), 1) // 16 == iota((elems, cols), 0)).astype(F32).astype(BF16)
    code = dot(code, spread).astype(jnp.int32)
    lane = iota((1, cols), 1)
    i, j = lane // 4 % 4, lane % 4

    def source(code, p):
        edge, q = code % 4, 3 - p
        si = jnp.where(edge == 0, 0, jnp.where(edge == 1, q, jnp.where(edge == 2, 3, 3 - q)))
        sj = jnp.where(edge == 0, q, jnp.where(edge == 1, 3, jnp.where(edge == 2, 3 - q, 0)))
        return code // 4 * 16 + si * 4 + sj

    across = jnp.where(i == 0, source(code[0:1], j), source(code[2:3], 3 - j))
    across = jnp.where((i == 0) | (i == 3), across, -1)
    along = jnp.where(j == 3, source(code[1:2], i), source(code[3:4], 3 - i))
    along = jnp.where((j == 0) | (j == 3), along, -1)
    own = 1.0 - 0.5 * ((across >= 0).astype(F32) + (along >= 0).astype(F32))

    def rows_of(start):
        row = iota((BLOCK, cols), 0) + start
        return jnp.where(row == across, 0.5, 0.0) + jnp.where(row == along, 0.5, 0.0)

    even = position % 2 == 0
    halo[:BLOCK] = rows_of(jnp.where(even, BLOCK + cols, 0)).astype(BF16)
    halo[BLOCK:] = rows_of(jnp.where(even, 0, BLOCK + cols)).astype(BF16)
    for r in range(0, cols, BLOCK):
        value = rows_of(BLOCK + r) + jnp.where(iota((BLOCK, cols), 0) + r == lane, own, 0.0)
        local[r : r + BLOCK] = value.astype(BF16)


def first_kernel(
    total, levels, tr, vel, metric, wide, fine, near, far, nb, ne,
    part, speed, local, halo, high, low,
):
    rows, cols = tr.shape
    scale = -STEP * metric[...]
    speed[...] = vel[...] * scale
    for b in range(BLOCK, cols - BLOCK, BLOCK):
        tile = slice(b, b + BLOCK)
        first = repeat_rows(speed[:levels, tile], rows // levels)
        second = repeat_rows(speed[levels:, tile], rows // levels)
        high[:, tile], low[:, tile] = split(advance(tr[:, tile], first, second, wide, fine))
    for start, value in zip(rim_starts(cols), (near, far), strict=True):
        tile = pl.ds(start, BLOCK)
        high[:, tile], low[:, tile] = split(value[...])
    build_assembly(total, lax.axis_index("sfc"), nb, ne, local, halo)
    part[...] = dot(high[...], local[...]) + dot(low[...], local[...])


def halo_parts(near, far):
    nh, nl = split(near)
    fh, fl = split(far)
    return jnp.concatenate([nh, fh], axis=1), jnp.concatenate([nl, fl], axis=1)


def rim2_kernel(
    levels, part, near, far, halo, wide, fine, tr, speed, heat, out_near, out_far, high, low
):
    rows, cols = part.shape
    high[...], low[...] = halo_parts(near[...], far[...])
    for start, out in zip(rim_starts(cols), (out_near, out_far), strict=True):
        tile = pl.ds(start, BLOCK)
        warm_tile = pl.ds(pl.multiple_of(jnp.where(start == 0, 0, BLOCK), BLOCK), BLOCK)
        section = part[:, tile] + dot(high[...], halo[:, tile]) + dot(low[...], halo[:, tile])
        first = repeat_rows(speed[:levels, tile], rows // levels)
        second = repeat_rows(speed[levels:, tile], rows // levels)
        field = 0.5 * (tr[:, tile] + advance(section, first, second, wide, fine))
        warm = (0.5 * STEP) * heat[:, warm_tile]
        out[:levels] = field[:levels] + warm
        out[levels:] = field[levels:]


def inner2_kernel(
    levels, part, high, low, halo, local, wide, fine, tr, speed, heat,
    own_near, own_far, out, own_high, own_low,
):
    rows, cols = part.shape
    inner = slice(BLOCK, cols - BLOCK)
    section = part[:, inner] + dot(high[...], halo[:, inner]) + dot(low[...], halo[:, inner])
    for b in range(BLOCK, cols - BLOCK, BLOCK):
        tile = slice(b, b + BLOCK)
        first = repeat_rows(speed[:levels, tile], rows // levels)
        second = repeat_rows(speed[levels:, tile], rows // levels)
        field = advance(section[:, b - BLOCK : b], first, second, wide, fine)
        field = 0.5 * (tr[:, tile] + field)
        warm = (0.5 * STEP) * heat[:, b - BLOCK : b]
        field = jnp.concatenate([field[:levels] + warm, field[levels:]], axis=0)
        own_high[:, tile], own_low[:, tile] = split(field)
    for start, value in zip(rim_starts(cols), (own_near, own_far), strict=True):
        tile = pl.ds(start, BLOCK)
        own_high[:, tile], own_low[:, tile] = split(value[...])
    out[...] = dot(own_high[...], local[...]) + dot(own_low[...], local[...])


def last_kernel(chunk, part, near, far, halo, heat_rim, heat_in, out_hbm, heat_hbm, out, sems):
    rows, cols = part.shape
    pairs = [
        (heat_rim.at[:, pl.ds(0, BLOCK)], heat_hbm.at[:, pl.ds(0, BLOCK)]),
        (heat_in, heat_hbm.at[:, pl.ds(BLOCK, cols - 2 * BLOCK)]),
        (heat_rim.at[:, pl.ds(BLOCK, BLOCK)], heat_hbm.at[:, pl.ds(cols - BLOCK, BLOCK)]),
    ]
    copies = [pltpu.make_async_copy(a, b, sems.at[k]) for k, (a, b) in enumerate(pairs)]
    for copy in copies:
        copy.start()
    for k, r0 in enumerate(range(0, rows, chunk)):
        r = pl.ds(r0, chunk)
        high, low = halo_parts(near[r], far[r])
        out[r] = part[r] + dot(high, halo[...]) + dot(low, halo[...])
        copy = pltpu.make_async_copy(out.at[r], out_hbm.at[r], sems.at[len(pairs) + k])
        copy.start()
        copies.append(copy)
    for copy in copies:
        copy.wait()


def heat_kernel(blocks, build, after, absorber, cosine, mass, absorption, flux, lit, *refs):
    if build:
        out, weights, depth, beams = refs
    else:
        weights, out, depth, beams = refs
    gases, levels, points = absorption.shape
    width = len(blocks) * BLOCK
    span = gases * levels

    if build:

        @pl.when(jnp.max(lit[...]) > 0)
        def _():
            table = absorption[...].astype(F32).reshape(span, points).T
            keep = iota((levels, span), 1) % levels <= iota((levels, span), 0)
            for g in range(points):
                weights[g * levels : (g + 1) * levels] = jnp.where(keep, table[g : g + 1], 0.0).astype(BF16)

    lanes = iota(lit.shape, 1)
    chosen = functools.reduce(jnp.logical_or, [lanes == b for b in blocks])
    any_lit = jnp.max(jnp.where(chosen, lit[...], 0))

    @pl.when(any_lit == 0)
    def _():
        out[...] = jnp.zeros_like(out)

    @pl.when(any_lit > 0)
    def _():
        beams[...] = jnp.broadcast_to(jnp.broadcast_to(flux[...], (8, points)).T[:, :1], beams.shape)
        amounts = jnp.concatenate([absorber[b * BLOCK : (b + 1) * BLOCK] for b in blocks], axis=0)
        cos = jnp.concatenate([cosine[:, b * BLOCK : (b + 1) * BLOCK] for b in blocks], axis=1)
        cos = cos.astype(F32)
        scale = jnp.broadcast_to(-math.log2(math.e) / cos, (8, width))
        depth[...] = dot(weights[...], amounts.T)
        strips = []
        for r in range(0, levels, 8):
            tiles = []
            for t in range(0, width, BLOCK):
                total = jnp.zeros((8, BLOCK), F32)
                for g in range(points):
                    d = depth[g * levels + r : g * levels + r + 8, t : t + BLOCK]
                    total = total + beams[g : g + 1] * jnp.exp2(d * scale[:, t : t + BLOCK])
                tiles.append(total)
            strips.append(jnp.concatenate(tiles, axis=1))
        down = jnp.concatenate(strips, axis=0)
        top = jnp.sum(beams[...], axis=0, keepdims=True)
        top = jnp.concatenate([top] * len(blocks), axis=1)
        above = jnp.concatenate([top, down[:-1]], axis=0)
        value = cos * (above - down)
        for k, b in enumerate(blocks):
            tile = slice(k * BLOCK, (k + 1) * BLOCK)
            on = jnp.max(jnp.where(lanes == b, lit[...], 0)).astype(F32)
            weight = mass[:, b * BLOCK : (b + 1) * BLOCK].astype(F32)
            out[:, tile] = on * value[:, tile] / weight


def struct(shape, dtype=F32):
    return pltpu.VMEM(shape, dtype)


def shards(
    tracers, velocity, metric, absorber, cosine, mass, absorption, flux, lit, neighbour, edge
):
    count, levels, cols = tracers.shape
    gases, points, _ = absorption.shape
    peers = lax.axis_size("sfc")
    total = neighbour.shape[1] * peers
    rows = count * levels
    pair = [(i, i ^ 1) for i in range(peers)]
    cross = [(i, (i + 2 * (i % 2) - 1) % peers) for i in range(peers)]
    tr = tracers.reshape(rows, cols)
    vel = velocity.reshape(2 * levels, cols)
    metric = metric.reshape(1, cols)
    absorption = absorption.transpose(0, 2, 1)
    flux = flux.reshape(1, points)
    lit = lit.reshape(1, -1)
    side = struct((rows, BLOCK))
    half = struct((rows, 2 * BLOCK), BF16)
    full = struct((rows, cols))

    def like(x):
        return struct(x.shape, x.dtype)

    moved = (tr, vel, metric, neighbour, edge, absorber, mass, absorption, flux, lit, cosine)
    near, far, wide, fine, *moved = pl.pallas_call(
        functools.partial(rim_kernel, levels),
        in_specs=[HBM] * len(moved),
        out_specs=[VMEM] * (4 + len(moved)),
        out_shape=[side, side, struct((2 * BLOCK, 2 * BLOCK), BF16), struct((BLOCK, 2 * BLOCK), BF16)]
        + [like(x) for x in moved],
        scratch_shapes=[pltpu.SemaphoreType.DMA((len(moved) + 4,))],
        compiler_params=params(),
        name="rims_first",
    )(*[pltpu.with_memory_space_constraint(x, pltpu.HBM) for x in moved])
    tr, vel, metric, neighbour, edge, absorber, mass, absorption, flux, lit, cosine = moved
    cosine = cosine.reshape(1, cols)
    from_far = lax.ppermute(far, "sfc", cross)
    from_near = lax.ppermute(near, "sfc", pair)

    weights = struct((points * levels, gases * levels), BF16)

    def heat(after, blocks, name, *extra):
        out = struct((levels, len(blocks) * BLOCK))
        return pl.pallas_call(
            functools.partial(heat_kernel, blocks, not extra),
            in_specs=[HBM] + [VMEM] * (6 + len(extra)),
            out_specs=VMEM if extra else [VMEM] * 2,
            out_shape=out if extra else [out, weights],
            scratch_shapes=[
                pltpu.VMEM((points * levels, len(blocks) * BLOCK), F32),
                pltpu.VMEM((points, BLOCK), F32),
            ],
            compiler_params=params(16),
            cost_estimate=cost(1e9),
            name=name,
        )(after, absorber, cosine, mass, absorption, flux, lit, *extra)

    part, speed, local, halo = pl.pallas_call(
        functools.partial(first_kernel, total, levels),
        in_specs=[VMEM] * 9,
        out_specs=[VMEM] * 4,
        out_shape=[
            full,
            struct((2 * levels, cols)),
            struct((cols, cols), BF16),
            struct((2 * BLOCK, cols), BF16),
        ],
        scratch_shapes=[pltpu.VMEM((rows, cols), BF16)] * 2,
        compiler_params=params(),
        cost_estimate=cost(1e9),
        name="first_local",
    )(tr, vel, metric, wide, fine, near, far, neighbour, edge)
    heat_rim, weights = heat(halo, (0, 3), "heat_rims")

    own_near, own_far, high, low = pl.pallas_call(
        functools.partial(rim2_kernel, levels),
        in_specs=[VMEM] * 9,
        out_specs=[VMEM] * 4,
        out_shape=[side, side, half, half],
        compiler_params=params(),
        name="rims_second",
    )(part, from_near, from_far, halo, wide, fine, tr, speed, heat_rim)
    next_far = lax.ppermute(own_far, "sfc", cross)
    next_near = lax.ppermute(own_near, "sfc", pair)
    heat_in = heat(high, (1, 2), "heat_inner", weights)
    part2 = pl.pallas_call(
        functools.partial(inner2_kernel, levels),
        in_specs=[VMEM] * 12,
        out_specs=VMEM,
        out_shape=full,
        scratch_shapes=[pltpu.VMEM((rows, cols), BF16)] * 2,
        compiler_params=params(),
        cost_estimate=cost(1e9),
        name="second_local",
    )(part, high, low, halo, local, wide, fine, tr, speed, heat_in, own_near, own_far)
    advanced, heating = pl.pallas_call(
        functools.partial(last_kernel, 2 * levels),
        in_specs=[VMEM] * 6,
        out_specs=[HBM] * 2,
        out_shape=[jax.ShapeDtypeStruct((rows, cols), F32), jax.ShapeDtypeStruct((levels, cols), F32)],
        scratch_shapes=[pltpu.VMEM((rows, cols), F32), pltpu.SemaphoreType.DMA((3 + count // 2,))],
        compiler_params=params(),
        name="last",
    )(part2, next_near, next_far, halo, heat_rim, heat_in)
    return advanced.reshape(tracers.shape), heating


def solution(mesh):
    placed = (
        P(None, None, ("grp", "sfc")),
        P(None, None, ("grp", "sfc")),
        P(("grp", "sfc")),
        P(("grp", "sfc"), None),
        P(("grp", "sfc")),
        P(None, ("grp", "sfc")),
        P(),
        P(),
        P(("grp", "sfc")),
        P(None, ("grp", "sfc")),
        P(None, ("grp", "sfc")),
    )
    return jax.shard_map(
        shards,
        mesh=mesh,
        in_specs=placed,
        out_specs=(P(None, None, ("grp", "sfc")), P(None, ("grp", "sfc"))),
        check_vma=False,
    )
```

```python
import functools
import math

import jax
import jax.numpy as jnp
import numpy as np
from jax import lax
from jax.experimental import pallas as pl
from jax.experimental.pallas import tpu as pltpu
from jax.sharding import PartitionSpec as P

BLOCK = 128
RIM = 8
STEP = 0.1
BITS = 21
LOWER = 32 - BITS
HALF = 1 << (BITS - 1)
SPAN = float(HALF - 8)
F32 = jnp.float32
BF16 = jnp.bfloat16
VMEM = pl.BlockSpec(memory_space=pltpu.VMEM)
SMEM = pl.BlockSpec(memory_space=pltpu.SMEM)
HBM = pl.BlockSpec(memory_space=pltpu.HBM)


def derivative_table():
    nodes = np.array([-1.0, -1.0 / math.sqrt(5.0), 1.0 / math.sqrt(5.0), 1.0])
    weights = np.array(
        [1.0 / np.prod([nodes[i] - nodes[m] for m in range(4) if m != i]) for i in range(4)]
    )
    table = np.zeros((4, 4))
    for i in range(4):
        for m in range(4):
            if i != m:
                table[i, m] = weights[m] / weights[i] / (nodes[i] - nodes[m])
        table[i, i] = -sum(table[i, m] for m in range(4) if m != i)
    return table


def params(mib=8):
    return pltpu.CompilerParams(vmem_limit_bytes=mib << 20)


def cost(flops, size=1 << 20):
    return pl.CostEstimate(flops=int(flops), bytes_accessed=int(size), transcendentals=0)


def iota(shape, dim):
    return lax.broadcasted_iota(jnp.int32, shape, dim)


def split(x):
    high = x.astype(BF16)
    return high, (x - high.astype(F32)).astype(BF16)


def dot(a, b):
    return jnp.dot(a, b, preferred_element_type=F32)


def build_derivatives(wide_ref, fine_ref):
    table = derivative_table()
    src, dst = iota((BLOCK, BLOCK), 0), iota((BLOCK, BLOCK), 1)
    si, sj, di, dj = src // 4 % 4, src % 4, dst // 4 % 4, dst % 4
    same = src // 16 == dst // 16
    halves = []
    for d, s, keep in ((di, si, same & (sj == dj)), (dj, sj, same & (si == di))):
        pick = jnp.where(keep, d * 4 + s, -1)
        value = jnp.zeros((BLOCK, BLOCK), F32)
        for i in range(4):
            for m in range(4):
                value = jnp.where(pick == i * 4 + m, float(table[i, m]), value)
        halves.append(value)
    high, low = split(jnp.concatenate(halves, axis=1))
    wide_ref[:BLOCK] = high
    wide_ref[BLOCK:] = high
    fine_ref[...] = low


def advance(field, first, second, wide_ref, fine_ref):
    high, low = split(field)
    both = dot(jnp.concatenate([high, low], axis=1), wide_ref[...]) + dot(high, fine_ref[...])
    return field + first * both[:, :BLOCK] + second * both[:, BLOCK:]


def repeat_rows(x, times):
    return jnp.concatenate([x] * times, axis=0) if times > 1 else x


def rim_starts(cols):
    near = jnp.where(lax.axis_index("sfc") % 2 == 0, cols - BLOCK, 0)
    return pl.multiple_of(near, BLOCK), pl.multiple_of(cols - BLOCK - near, BLOCK)


def rim_kernel(levels, *refs):
    count = (len(refs) - 5) // 2
    given, (sent, far, wide, fine), kept, sems = (
        refs[:count], refs[count : count + 4], refs[count + 4 : -1], refs[-1],
    )
    tr_hbm, vel_hbm, metric_hbm = given[:3]
    tr, vel, metric = kept[:3]
    rows, cols = tr.shape
    rims = [pl.ds(start, BLOCK) for start in rim_starts(cols)[::-1]]
    inner = pl.ds(BLOCK, cols - 2 * BLOCK)
    pairs = [(metric_hbm, metric)]
    pairs += [(hbm.at[:, r], ref.at[:, r]) for r in rims for hbm, ref in ((vel_hbm, vel), (tr_hbm, tr))]
    pairs += [(hbm.at[:, inner], ref.at[:, inner]) for hbm, ref in ((vel_hbm, vel), (tr_hbm, tr))]
    pairs += list(zip(given[3:], kept[3:], strict=True))
    copies = [pltpu.make_async_copy(a, b, sems.at[k]) for k, (a, b) in enumerate(pairs)]
    for copy in copies:
        copy.start()
    build_derivatives(wide, fine)
    copies[0].wait()
    for copy in copies[1:3]:
        copy.wait()
    rim = rims[0]
    scale = -STEP * metric[:, rim]
    first = repeat_rows(vel[:levels, rim] * scale, rows // levels)
    second = repeat_rows(vel[levels:, rim] * scale, rows // levels)
    field = advance(tr[:, rim], first, second, wide, fine)
    far[...] = field
    sent[...] = encode(field)
    for copy in copies[3:]:
        copy.wait()


def near_kernel(levels, tr, vel, metric, wide, fine, sent, near):
    rows, cols = tr.shape
    rim = pl.ds(rim_starts(cols)[0], BLOCK)
    scale = -STEP * metric[:, rim]
    first = repeat_rows(vel[:levels, rim] * scale, rows // levels)
    second = repeat_rows(vel[levels:, rim] * scale, rows // levels)
    field = advance(tr[:, rim], first, second, wide, fine)
    near[...] = field
    sent[...] = encode(field)


def is_point(shape, *points):
    point = iota(shape, 1) % 16
    return functools.reduce(jnp.logical_or, [point == p for p in points])


def shifted(x, shift):
    return pltpu.roll(x, shift % BLOCK, 1)


def pack(rim):
    size = rim.shape[0] // 4
    a, b, c, d = (rim[k * size : (k + 1) * size] for k in range(4))
    shape = d.shape
    upper = is_point(shape, 5, 6)
    moved = (
        jnp.where(upper, shifted(d, 5), shifted(d, 7)),
        jnp.where(upper, shifted(d, -7), shifted(d, -5)),
        jnp.where(is_point(shape, 5, 9), shifted(d, 1), shifted(d, -1)),
    )
    inside = is_point(shape, 5, 6, 9, 10)
    return jnp.concatenate([jnp.where(inside, m, x) for m, x in zip(moved, (a, b, c), strict=True)], axis=0)


def encode(rim):
    packed = pack(rim)
    strips = [packed[r : r + 8] for r in range(0, packed.shape[0], 8)]
    largest = functools.reduce(jnp.maximum, [jnp.abs(x) for x in strips])
    power = jnp.clip(jnp.ceil(jnp.log2(largest)), -125.0, 125.0)
    scale = jnp.exp2(-power)
    count = len(strips) // 3
    words = [(x * scale * SPAN + (HALF + 0.5)).astype(jnp.int32) for x in strips]
    a, b, c = (words[k * count : (k + 1) * count] for k in range(3))
    first = [x | (z << BITS) for x, z in zip(a, c, strict=True)]
    second = [y | ((z >> LOWER) << BITS) for y, z in zip(b, c, strict=True)]
    return jnp.concatenate([power.astype(jnp.int32)] + first + second, axis=0)


def decode(sent):
    scale = jnp.exp2(sent[:8].astype(F32)) * (1.0 / SPAN)
    count = (sent.shape[0] - 8) // 16
    words = [sent[8 + r * 8 : 16 + r * 8] for r in range(2 * count)]
    a, b, c = [], [], []
    for first, second in zip(words[:count], words[count:], strict=True):
        a.append(first & (2 * HALF - 1))
        b.append(second & (2 * HALF - 1))
        upper = lax.shift_right_logical(second, BITS) << LOWER
        c.append(lax.shift_right_logical(first, BITS) | upper)
    return unpack(jnp.concatenate([(x - HALF).astype(F32) * scale for x in a + b + c], axis=0))


def unpack(sent):
    size = sent.shape[0] // 3
    a, b, c = (sent[k * size : (k + 1) * size] for k in range(3))
    shape = a.shape
    d = jnp.where(is_point(shape, 4, 8), shifted(c, -1), shifted(c, 1))
    d = jnp.where(is_point(shape, 0, 1), shifted(a, -5), d)
    d = jnp.where(is_point(shape, 2, 3), shifted(a, -7), d)
    d = jnp.where(is_point(shape, 12, 13), shifted(b, 7), d)
    d = jnp.where(is_point(shape, 14, 15), shifted(b, 5), d)
    return jnp.concatenate([a, b, c, d], axis=0)


def build_assembly(total, position, nb, ne, local, halo):
    elems, cols = nb.shape[1], local.shape[1]
    index = nb[...] - position * elems + RIM
    index = jnp.where(index < 0, index + total, index)
    index = jnp.where(index >= total, index - total, index)
    code = (index * 4 + ne[...]).astype(F32).astype(BF16)
    spread = (iota((elems, cols), 1) // 16 == iota((elems, cols), 0)).astype(F32).astype(BF16)
    code = dot(code, spread).astype(jnp.int32)
    lane = iota((1, cols), 1)
    i, j = lane // 4 % 4, lane % 4

    def source(code, p):
        edge, q = code % 4, 3 - p
        si = jnp.where(edge == 0, 0, jnp.where(edge == 1, q, jnp.where(edge == 2, 3, 3 - q)))
        sj = jnp.where(edge == 0, q, jnp.where(edge == 1, 3, jnp.where(edge == 2, 3 - q, 0)))
        return code // 4 * 16 + si * 4 + sj

    across = jnp.where(i == 0, source(code[0:1], j), source(code[2:3], 3 - j))
    across = jnp.where((i == 0) | (i == 3), across, -1)
    along = jnp.where(j == 3, source(code[1:2], i), source(code[3:4], 3 - i))
    along = jnp.where((j == 0) | (j == 3), along, -1)
    own = 1.0 - 0.5 * ((across >= 0).astype(F32) + (along >= 0).astype(F32))

    def rows_of(start):
        row = iota((BLOCK, cols), 0) + start
        return jnp.where(row == across, 0.5, 0.0) + jnp.where(row == along, 0.5, 0.0)

    even = position % 2 == 0
    halo[:BLOCK] = rows_of(jnp.where(even, BLOCK + cols, 0)).astype(BF16)
    halo[BLOCK:] = rows_of(jnp.where(even, 0, BLOCK + cols)).astype(BF16)
    for r in range(0, cols, BLOCK):
        value = rows_of(BLOCK + r) + jnp.where(iota((BLOCK, cols), 0) + r == lane, own, 0.0)
        local[r : r + BLOCK] = value.astype(BF16)


def first_kernel(
    total, levels, tr, vel, metric, wide, fine, near, far, nb, ne,
    part, speed, local, halo, high, low,
):
    rows, cols = tr.shape
    scale = -STEP * metric[...]
    speed[...] = vel[...] * scale
    for b in range(BLOCK, cols - BLOCK, BLOCK):
        tile = slice(b, b + BLOCK)
        first = repeat_rows(speed[:levels, tile], rows // levels)
        second = repeat_rows(speed[levels:, tile], rows // levels)
        high[:, tile], low[:, tile] = split(advance(tr[:, tile], first, second, wide, fine))
    for start, value in zip(rim_starts(cols), (near, far), strict=True):
        tile = pl.ds(start, BLOCK)
        high[:, tile], low[:, tile] = split(value[...])
    build_assembly(total, lax.axis_index("sfc"), nb, ne, local, halo)
    part[...] = dot(high[...], local[...]) + dot(low[...], local[...])


def halo_parts(near, far):
    nh, nl = split(near)
    fh, fl = split(far)
    return jnp.concatenate([nh, fh], axis=1), jnp.concatenate([nl, fl], axis=1)


def second_rim(levels, start, part, high, low, halo, wide, fine, tr, speed, heat):
    rows, cols = part.shape
    tile = pl.ds(start, BLOCK)
    warm_tile = pl.ds(pl.multiple_of(jnp.where(start == 0, 0, BLOCK), BLOCK), BLOCK)
    section = part[:, tile] + dot(high[...], halo[:, tile]) + dot(low[...], halo[:, tile])
    first = repeat_rows(speed[:levels, tile], rows // levels)
    second = repeat_rows(speed[levels:, tile], rows // levels)
    field = 0.5 * (tr[:, tile] + advance(section, first, second, wide, fine))
    warm = (0.5 * STEP) * heat[:, warm_tile]
    return jnp.concatenate([field[:levels] + warm, field[levels:]], axis=0)


def far2_kernel(
    levels, part, near, sent, halo, wide, fine, tr, speed, heat, out_sent, out_far, high, low
):
    high[...], low[...] = halo_parts(decode(near[...]), decode(sent[...]))
    start = rim_starts(part.shape[1])[1]
    field = second_rim(levels, start, part, high, low, halo, wide, fine, tr, speed, heat)
    out_far[...] = field
    out_sent[...] = encode(field)


def near2_kernel(levels, part, high, low, halo, wide, fine, tr, speed, heat, sent, out):
    start = rim_starts(part.shape[1])[0]
    out[...] = second_rim(levels, start, part, high, low, halo, wide, fine, tr, speed, heat)
    sent[...] = encode(out[...])


def inner2_kernel(
    levels, part, high, low, halo, local, wide, fine, tr, speed, heat,
    own_near, own_far, out, own_high, own_low,
):
    rows, cols = part.shape
    inner = slice(BLOCK, cols - BLOCK)
    section = part[:, inner] + dot(high[...], halo[:, inner]) + dot(low[...], halo[:, inner])
    for b in range(BLOCK, cols - BLOCK, BLOCK):
        tile = slice(b, b + BLOCK)
        first = repeat_rows(speed[:levels, tile], rows // levels)
        second = repeat_rows(speed[levels:, tile], rows // levels)
        field = advance(section[:, b - BLOCK : b], first, second, wide, fine)
        field = 0.5 * (tr[:, tile] + field)
        warm = (0.5 * STEP) * heat[:, b - BLOCK : b]
        field = jnp.concatenate([field[:levels] + warm, field[levels:]], axis=0)
        own_high[:, tile], own_low[:, tile] = split(field)
    for start, value in zip(rim_starts(cols), (own_near, own_far), strict=True):
        tile = pl.ds(start, BLOCK)
        own_high[:, tile], own_low[:, tile] = split(value[...])
    out[...] = dot(own_high[...], local[...]) + dot(own_low[...], local[...])


def last_kernel(chunk, part, near, far, halo, heat_rim, heat_in, out_hbm, heat_hbm, out, sems):
    rows, cols = part.shape
    pairs = [
        (heat_rim.at[:, pl.ds(0, BLOCK)], heat_hbm.at[:, pl.ds(0, BLOCK)]),
        (heat_in, heat_hbm.at[:, pl.ds(BLOCK, cols - 2 * BLOCK)]),
        (heat_rim.at[:, pl.ds(BLOCK, BLOCK)], heat_hbm.at[:, pl.ds(cols - BLOCK, BLOCK)]),
    ]
    copies = [pltpu.make_async_copy(a, b, sems.at[k]) for k, (a, b) in enumerate(pairs)]
    for copy in copies:
        copy.start()
    whole_near, whole_far = decode(near[...]), decode(far[...])
    for k, r0 in enumerate(range(0, rows, chunk)):
        r = pl.ds(r0, chunk)
        high, low = halo_parts(whole_near[r0 : r0 + chunk], whole_far[r0 : r0 + chunk])
        out[r] = part[r] + dot(high, halo[...]) + dot(low, halo[...])
        copy = pltpu.make_async_copy(out.at[r], out_hbm.at[r], sems.at[len(pairs) + k])
        copy.start()
        copies.append(copy)
    for copy in copies:
        copy.wait()


def heat_kernel(blocks, build, after, absorber, cosine, mass, absorption, flux, lit, *refs):
    if build:
        out, weights, depth, beams = refs
    else:
        weights, out, depth, beams = refs
    gases, levels, points = absorption.shape
    width = len(blocks) * BLOCK
    span = gases * levels

    if build:

        @pl.when(jnp.max(lit[...]) > 0)
        def _():
            table = absorption[...].astype(F32).reshape(span, points).T
            keep = iota((levels, span), 1) % levels <= iota((levels, span), 0)
            for g in range(points):
                weights[g * levels : (g + 1) * levels] = jnp.where(keep, table[g : g + 1], 0.0).astype(BF16)

    lanes = iota(lit.shape, 1)
    chosen = functools.reduce(jnp.logical_or, [lanes == b for b in blocks])
    any_lit = jnp.max(jnp.where(chosen, lit[...], 0))

    @pl.when(any_lit == 0)
    def _():
        out[...] = jnp.zeros_like(out)

    @pl.when(any_lit > 0)
    def _():
        beams[...] = jnp.broadcast_to(jnp.broadcast_to(flux[...], (8, points)).T[:, :1], beams.shape)
        amounts = jnp.concatenate([absorber[b * BLOCK : (b + 1) * BLOCK] for b in blocks], axis=0)
        cos = jnp.concatenate([cosine[:, b * BLOCK : (b + 1) * BLOCK] for b in blocks], axis=1)
        cos = cos.astype(F32)
        scale = jnp.broadcast_to(-math.log2(math.e) / cos, (8, width))
        depth[...] = dot(weights[...], amounts.T)
        strips = range(0, levels, 8)
        tiles = range(0, width, BLOCK)
        totals = {(r, t): jnp.zeros((8, BLOCK), F32) for r in strips for t in tiles}
        for g in range(points):
            beam = jnp.broadcast_to(beams[g : g + 1], (8, BLOCK))
            for r, t in totals:
                d = depth[g * levels + r : g * levels + r + 8, t : t + BLOCK]
                totals[r, t] += beam * jnp.exp2(d * scale[:, t : t + BLOCK])
        down = [jnp.concatenate([totals[r, t] for r in strips], axis=0) for t in tiles]
        down = jnp.concatenate(down, axis=1)
        top = jnp.sum(beams[...], axis=0, keepdims=True)
        top = jnp.concatenate([top] * len(blocks), axis=1)
        above = jnp.concatenate([top, down[:-1]], axis=0)
        value = cos * (above - down)
        for k, b in enumerate(blocks):
            tile = slice(k * BLOCK, (k + 1) * BLOCK)
            on = jnp.max(jnp.where(lanes == b, lit[...], 0)).astype(F32)
            weight = mass[:, b * BLOCK : (b + 1) * BLOCK].astype(F32)
            out[:, tile] = on * value[:, tile] / weight


def struct(shape, dtype=F32):
    return pltpu.VMEM(shape, dtype)


def shards(
    tracers, velocity, metric, absorber, cosine, mass, absorption, flux, lit, neighbour, edge
):
    count, levels, cols = tracers.shape
    gases, points, _ = absorption.shape
    peers = lax.axis_size("sfc")
    total = neighbour.shape[1] * peers
    rows = count * levels
    pair = [(i, i ^ 1) for i in range(peers)]
    cross = [(i, (i + 2 * (i % 2) - 1) % peers) for i in range(peers)]
    tr = tracers.reshape(rows, cols)
    vel = velocity.reshape(2 * levels, cols)
    metric = metric.reshape(1, cols)
    absorption = absorption.transpose(0, 2, 1)
    flux = flux.reshape(1, points)
    lit = lit.reshape(1, -1)
    side = struct((rows, BLOCK))
    packed = struct((rows // 2 + 8, BLOCK), jnp.int32)
    half = struct((rows, 2 * BLOCK), BF16)
    full = struct((rows, cols))

    def like(x):
        return struct(x.shape, x.dtype)

    moved = (tr, vel, metric, neighbour, edge, absorber, mass, absorption, flux, lit, cosine)
    sent, far, wide, fine, *moved = pl.pallas_call(
        functools.partial(rim_kernel, levels),
        in_specs=[HBM] * len(moved),
        out_specs=[VMEM] * (4 + len(moved)),
        out_shape=[packed, side, struct((2 * BLOCK, 2 * BLOCK), BF16), struct((BLOCK, 2 * BLOCK), BF16)]
        + [like(x) for x in moved],
        scratch_shapes=[pltpu.SemaphoreType.DMA((len(moved) + 4,))],
        compiler_params=params(),
        name="rims_first",
    )(*[pltpu.with_memory_space_constraint(x, pltpu.HBM) for x in moved])
    tr, vel, metric, neighbour, edge, absorber, mass, absorption, flux, lit, cosine = moved
    cosine = cosine.reshape(1, cols)
    from_far = lax.ppermute(sent, "sfc", cross)
    sent, near = pl.pallas_call(
        functools.partial(near_kernel, levels),
        in_specs=[VMEM] * 5,
        out_specs=[VMEM] * 2,
        out_shape=[packed, side],
        compiler_params=params(),
        name="near_first",
    )(tr, vel, metric, wide, fine)
    from_near = lax.ppermute(sent, "sfc", pair)

    weights = struct((points * levels, gases * levels), BF16)

    def heat(after, blocks, name, *extra):
        out = struct((levels, len(blocks) * BLOCK))
        return pl.pallas_call(
            functools.partial(heat_kernel, blocks, not extra),
            in_specs=[HBM] + [VMEM] * (6 + len(extra)),
            out_specs=VMEM if extra else [VMEM] * 2,
            out_shape=out if extra else [out, weights],
            scratch_shapes=[
                pltpu.VMEM((points * levels, len(blocks) * BLOCK), F32),
                pltpu.VMEM((points, BLOCK), F32),
            ],
            compiler_params=params(16),
            cost_estimate=cost(1e9),
            name=name,
        )(after, absorber, cosine, mass, absorption, flux, lit, *extra)

    part, speed, local, halo = pl.pallas_call(
        functools.partial(first_kernel, total, levels),
        in_specs=[VMEM] * 9,
        out_specs=[VMEM] * 4,
        out_shape=[
            full,
            struct((2 * levels, cols)),
            struct((cols, cols), BF16),
            struct((2 * BLOCK, cols), BF16),
        ],
        scratch_shapes=[pltpu.VMEM((rows, cols), BF16)] * 2,
        compiler_params=params(),
        cost_estimate=cost(1e9),
        name="first_local",
    )(tr, vel, metric, wide, fine, near, far, neighbour, edge)
    heat_rim, weights = heat(halo, (0, 3), "heat_rims")

    own_sent, own_far, high, low = pl.pallas_call(
        functools.partial(far2_kernel, levels),
        in_specs=[VMEM] * 9,
        out_specs=[VMEM] * 4,
        out_shape=[packed, side, half, half],
        compiler_params=params(),
        name="far_second",
    )(part, from_near, from_far, halo, wide, fine, tr, speed, heat_rim)
    next_far = lax.ppermute(own_sent, "sfc", cross)
    own_sent, own_near = pl.pallas_call(
        functools.partial(near2_kernel, levels),
        in_specs=[VMEM] * 9,
        out_specs=[VMEM] * 2,
        out_shape=[packed, side],
        compiler_params=params(),
        name="near_second",
    )(part, high, low, halo, wide, fine, tr, speed, heat_rim)
    next_near = lax.ppermute(own_sent, "sfc", pair)
    heat_in = heat(high, (1, 2), "heat_inner", weights)
    part2 = pl.pallas_call(
        functools.partial(inner2_kernel, levels),
        in_specs=[VMEM] * 12,
        out_specs=VMEM,
        out_shape=full,
        scratch_shapes=[pltpu.VMEM((rows, cols), BF16)] * 2,
        compiler_params=params(),
        cost_estimate=cost(1e9),
        name="second_local",
    )(part, high, low, halo, local, wide, fine, tr, speed, heat_in, own_near, own_far)
    advanced, heating = pl.pallas_call(
        functools.partial(last_kernel, 2 * levels),
        in_specs=[VMEM] * 6,
        out_specs=[HBM] * 2,
        out_shape=[jax.ShapeDtypeStruct((rows, cols), F32), jax.ShapeDtypeStruct((levels, cols), F32)],
        scratch_shapes=[pltpu.VMEM((rows, cols), F32), pltpu.SemaphoreType.DMA((3 + count // 2,))],
        compiler_params=params(),
        name="last",
    )(part2, next_near, next_far, halo, heat_rim, heat_in)
    return advanced.reshape(tracers.shape), heating


def solution(mesh):
    placed = (
        P(None, None, ("grp", "sfc")),
        P(None, None, ("grp", "sfc")),
        P(("grp", "sfc")),
        P(("grp", "sfc"), None),
        P(("grp", "sfc")),
        P(None, ("grp", "sfc")),
        P(),
        P(),
        P(("grp", "sfc")),
        P(None, ("grp", "sfc")),
        P(None, ("grp", "sfc")),
    )
    return jax.shard_map(
        shards,
        mesh=mesh,
        in_specs=placed,
        out_specs=(P(None, None, ("grp", "sfc")), P(None, ("grp", "sfc"))),
        check_vma=False,
    )
```

```python
import functools
import math

import jax
import jax.numpy as jnp
import numpy as np
from jax import lax
from jax.experimental import pallas as pl
from jax.experimental.pallas import tpu as pltpu
from jax.sharding import PartitionSpec as P

BLOCK = 128
RIM = 8
STEP = 0.1
BITS = 21
LOWER = 32 - BITS
HALF = 1 << (BITS - 1)
SPAN = float(HALF - 8)
F32 = jnp.float32
BF16 = jnp.bfloat16
VMEM = pl.BlockSpec(memory_space=pltpu.VMEM)
SMEM = pl.BlockSpec(memory_space=pltpu.SMEM)
HBM = pl.BlockSpec(memory_space=pltpu.HBM)


def derivative_table():
    nodes = np.array([-1.0, -1.0 / math.sqrt(5.0), 1.0 / math.sqrt(5.0), 1.0])
    weights = np.array(
        [1.0 / np.prod([nodes[i] - nodes[m] for m in range(4) if m != i]) for i in range(4)]
    )
    table = np.zeros((4, 4))
    for i in range(4):
        for m in range(4):
            if i != m:
                table[i, m] = weights[m] / weights[i] / (nodes[i] - nodes[m])
        table[i, i] = -sum(table[i, m] for m in range(4) if m != i)
    return table


def params(mib=8):
    return pltpu.CompilerParams(vmem_limit_bytes=mib << 20)


def cost(flops, size=1 << 20):
    return pl.CostEstimate(flops=int(flops), bytes_accessed=int(size), transcendentals=0)


def iota(shape, dim):
    return lax.broadcasted_iota(jnp.int32, shape, dim)


def split(x):
    high = x.astype(BF16)
    return high, (x - high.astype(F32)).astype(BF16)


def dot(a, b):
    return jnp.dot(a, b, preferred_element_type=F32)


def build_derivatives(wide_ref, fine_ref):
    table = derivative_table()
    src, dst = iota((BLOCK, BLOCK), 0), iota((BLOCK, BLOCK), 1)
    si, sj, di, dj = src // 4 % 4, src % 4, dst // 4 % 4, dst % 4
    same = src // 16 == dst // 16
    halves = []
    for d, s, keep in ((di, si, same & (sj == dj)), (dj, sj, same & (si == di))):
        pick = jnp.where(keep, d * 4 + s, -1)
        value = jnp.zeros((BLOCK, BLOCK), F32)
        for i in range(4):
            for m in range(4):
                value = jnp.where(pick == i * 4 + m, float(table[i, m]), value)
        halves.append(value)
    high, low = split(jnp.concatenate(halves, axis=1))
    wide_ref[:BLOCK] = high
    wide_ref[BLOCK:] = high
    fine_ref[...] = low


def advance(field, first, second, wide_ref, fine_ref):
    high, low = split(field)
    both = dot(jnp.concatenate([high, low], axis=1), wide_ref[...]) + dot(high, fine_ref[...])
    return field + first * both[:, :BLOCK] + second * both[:, BLOCK:]


def repeat_rows(x, times):
    return jnp.concatenate([x] * times, axis=0) if times > 1 else x


def rim_starts(cols):
    near = jnp.where(lax.axis_index("sfc") % 2 == 0, cols - BLOCK, 0)
    return pl.multiple_of(near, BLOCK), pl.multiple_of(cols - BLOCK - near, BLOCK)


def rim_kernel(levels, *refs):
    count = (len(refs) - 5) // 2
    given, (sent, far, wide, fine), kept, sems = (
        refs[:count], refs[count : count + 4], refs[count + 4 : -1], refs[-1],
    )
    tr_hbm, vel_hbm, metric_hbm = given[:3]
    tr, vel, metric = kept[:3]
    rows, cols = tr.shape
    rims = [pl.ds(start, BLOCK) for start in rim_starts(cols)[::-1]]
    inner = pl.ds(BLOCK, cols - 2 * BLOCK)
    pairs = [(metric_hbm, metric)]
    pairs += [(hbm.at[:, r], ref.at[:, r]) for r in rims for hbm, ref in ((vel_hbm, vel), (tr_hbm, tr))]
    pairs += [(hbm.at[:, inner], ref.at[:, inner]) for hbm, ref in ((vel_hbm, vel), (tr_hbm, tr))]
    pairs += list(zip(given[3:], kept[3:], strict=True))
    copies = [pltpu.make_async_copy(a, b, sems.at[k]) for k, (a, b) in enumerate(pairs)]
    for copy in copies:
        copy.start()
    build_derivatives(wide, fine)
    copies[0].wait()
    for copy in copies[1:3]:
        copy.wait()
    rim = rims[0]
    scale = -STEP * metric[:, rim]
    first = repeat_rows(vel[:levels, rim] * scale, rows // levels)
    second = repeat_rows(vel[levels:, rim] * scale, rows // levels)
    field = advance(tr[:, rim], first, second, wide, fine)
    far[...] = field
    sent[...] = encode(field)
    for copy in copies[3:]:
        copy.wait()


def is_point(shape, *points):
    point = iota(shape, 1) % 16
    return functools.reduce(jnp.logical_or, [point == p for p in points])


def shifted(x, shift):
    return pltpu.roll(x, shift % BLOCK, 1)


def pack(rim):
    size = rim.shape[0] // 4
    a, b, c, d = (rim[k * size : (k + 1) * size] for k in range(4))
    shape = d.shape
    upper = is_point(shape, 5, 6)
    moved = (
        jnp.where(upper, shifted(d, 5), shifted(d, 7)),
        jnp.where(upper, shifted(d, -7), shifted(d, -5)),
        jnp.where(is_point(shape, 5, 9), shifted(d, 1), shifted(d, -1)),
    )
    inside = is_point(shape, 5, 6, 9, 10)
    return jnp.concatenate([jnp.where(inside, m, x) for m, x in zip(moved, (a, b, c), strict=True)], axis=0)


def encode(rim):
    packed = pack(rim)
    strips = [packed[r : r + 8] for r in range(0, packed.shape[0], 8)]
    largest = functools.reduce(jnp.maximum, [jnp.abs(x) for x in strips])
    power = jnp.clip(jnp.ceil(jnp.log2(largest)), -125.0, 125.0)
    scale = jnp.exp2(-power)
    count = len(strips) // 3
    words = [(x * scale * SPAN + (HALF + 0.5)).astype(jnp.int32) for x in strips]
    a, b, c = (words[k * count : (k + 1) * count] for k in range(3))
    first = [x | (z << BITS) for x, z in zip(a, c, strict=True)]
    second = [y | ((z >> LOWER) << BITS) for y, z in zip(b, c, strict=True)]
    return jnp.concatenate([power.astype(jnp.int32)] + first + second, axis=0)


def decode(sent):
    scale = jnp.exp2(sent[:8].astype(F32)) * (1.0 / SPAN)
    count = (sent.shape[0] - 8) // 16
    words = [sent[8 + r * 8 : 16 + r * 8] for r in range(2 * count)]
    a, b, c = [], [], []
    for first, second in zip(words[:count], words[count:], strict=True):
        a.append(first & (2 * HALF - 1))
        b.append(second & (2 * HALF - 1))
        upper = lax.shift_right_logical(second, BITS) << LOWER
        c.append(lax.shift_right_logical(first, BITS) | upper)
    return unpack(jnp.concatenate([(x - HALF).astype(F32) * scale for x in a + b + c], axis=0))


def unpack(sent):
    size = sent.shape[0] // 3
    a, b, c = (sent[k * size : (k + 1) * size] for k in range(3))
    shape = a.shape
    d = jnp.where(is_point(shape, 4, 8), shifted(c, -1), shifted(c, 1))
    d = jnp.where(is_point(shape, 0, 1), shifted(a, -5), d)
    d = jnp.where(is_point(shape, 2, 3), shifted(a, -7), d)
    d = jnp.where(is_point(shape, 12, 13), shifted(b, 7), d)
    d = jnp.where(is_point(shape, 14, 15), shifted(b, 5), d)
    return jnp.concatenate([a, b, c, d], axis=0)


def build_assembly(total, position, nb, ne, local, halo):
    elems, cols = nb.shape[1], local.shape[1]
    index = nb[...] - position * elems + RIM
    index = jnp.where(index < 0, index + total, index)
    index = jnp.where(index >= total, index - total, index)
    code = (index * 4 + ne[...]).astype(F32).astype(BF16)
    spread = (iota((elems, cols), 1) // 16 == iota((elems, cols), 0)).astype(F32).astype(BF16)
    code = dot(code, spread).astype(jnp.int32)
    lane = iota((1, cols), 1)
    i, j = lane // 4 % 4, lane % 4

    def source(code, p):
        edge, q = code % 4, 3 - p
        si = jnp.where(edge == 0, 0, jnp.where(edge == 1, q, jnp.where(edge == 2, 3, 3 - q)))
        sj = jnp.where(edge == 0, q, jnp.where(edge == 1, 3, jnp.where(edge == 2, 3 - q, 0)))
        return code // 4 * 16 + si * 4 + sj

    across = jnp.where(i == 0, source(code[0:1], j), source(code[2:3], 3 - j))
    across = jnp.where((i == 0) | (i == 3), across, -1)
    along = jnp.where(j == 3, source(code[1:2], i), source(code[3:4], 3 - i))
    along = jnp.where((j == 0) | (j == 3), along, -1)
    own = 1.0 - 0.5 * ((across >= 0).astype(F32) + (along >= 0).astype(F32))

    def rows_of(start):
        row = iota((BLOCK, cols), 0) + start
        return jnp.where(row == across, 0.5, 0.0) + jnp.where(row == along, 0.5, 0.0)

    even = position % 2 == 0
    halo[:BLOCK] = rows_of(jnp.where(even, BLOCK + cols, 0)).astype(BF16)
    halo[BLOCK:] = rows_of(jnp.where(even, 0, BLOCK + cols)).astype(BF16)
    for r in range(0, cols, BLOCK):
        value = rows_of(BLOCK + r) + jnp.where(iota((BLOCK, cols), 0) + r == lane, own, 0.0)
        local[r : r + BLOCK] = value.astype(BF16)


def first_kernel(
    total, levels, tr, vel, metric, wide, fine, far, nb, ne,
    sent, part, speed, local, halo, high, low,
):
    rows, cols = tr.shape
    scale = -STEP * metric[...]
    speed[...] = vel[...] * scale
    near_start, far_start = rim_starts(cols)
    for start in (near_start, *range(BLOCK, cols - BLOCK, BLOCK)):
        tile = pl.ds(start, BLOCK)
        first = repeat_rows(speed[:levels, tile], rows // levels)
        second = repeat_rows(speed[levels:, tile], rows // levels)
        field = advance(tr[:, tile], first, second, wide, fine)
        if start is near_start:
            sent[...] = encode(field)
        high[:, tile], low[:, tile] = split(field)
    tile = pl.ds(far_start, BLOCK)
    high[:, tile], low[:, tile] = split(far[...])
    build_assembly(total, lax.axis_index("sfc"), nb, ne, local, halo)
    part[...] = dot(high[...], local[...]) + dot(low[...], local[...])


def halo_parts(near, far):
    nh, nl = split(near)
    fh, fl = split(far)
    return jnp.concatenate([nh, fh], axis=1), jnp.concatenate([nl, fl], axis=1)


def second_rim(levels, start, part, high, low, halo, wide, fine, tr, speed, heat):
    rows, cols = part.shape
    tile = pl.ds(start, BLOCK)
    warm_tile = pl.ds(pl.multiple_of(jnp.where(start == 0, 0, BLOCK), BLOCK), BLOCK)
    section = part[:, tile] + dot(high[...], halo[:, tile]) + dot(low[...], halo[:, tile])
    first = repeat_rows(speed[:levels, tile], rows // levels)
    second = repeat_rows(speed[levels:, tile], rows // levels)
    field = 0.5 * (tr[:, tile] + advance(section, first, second, wide, fine))
    warm = (0.5 * STEP) * heat[:, warm_tile]
    return jnp.concatenate([field[:levels] + warm, field[levels:]], axis=0)


def far2_kernel(
    levels, part, near, sent, halo, wide, fine, tr, speed, heat, out_sent, out_far, high, low
):
    high[...], low[...] = halo_parts(decode(near[...]), decode(sent[...]))
    start = rim_starts(part.shape[1])[1]
    field = second_rim(levels, start, part, high, low, halo, wide, fine, tr, speed, heat)
    out_far[...] = field
    out_sent[...] = encode(field)


def near2_kernel(levels, part, high, low, halo, wide, fine, tr, speed, heat, sent, out):
    start = rim_starts(part.shape[1])[0]
    out[...] = second_rim(levels, start, part, high, low, halo, wide, fine, tr, speed, heat)
    sent[...] = encode(out[...])


def inner2_kernel(
    levels, part, high, low, halo, local, wide, fine, tr, speed, heat,
    own_near, own_far, out, own_high, own_low,
):
    rows, cols = part.shape
    inner = slice(BLOCK, cols - BLOCK)
    section = part[:, inner] + dot(high[...], halo[:, inner]) + dot(low[...], halo[:, inner])
    for b in range(BLOCK, cols - BLOCK, BLOCK):
        tile = slice(b, b + BLOCK)
        first = repeat_rows(speed[:levels, tile], rows // levels)
        second = repeat_rows(speed[levels:, tile], rows // levels)
        field = advance(section[:, b - BLOCK : b], first, second, wide, fine)
        field = 0.5 * (tr[:, tile] + field)
        warm = (0.5 * STEP) * heat[:, b - BLOCK : b]
        field = jnp.concatenate([field[:levels] + warm, field[levels:]], axis=0)
        own_high[:, tile], own_low[:, tile] = split(field)
    for start, value in zip(rim_starts(cols), (own_near, own_far), strict=True):
        tile = pl.ds(start, BLOCK)
        own_high[:, tile], own_low[:, tile] = split(value[...])
    out[...] = dot(own_high[...], local[...]) + dot(own_low[...], local[...])


def last_kernel(chunk, part, near, far, halo, heat_rim, heat_in, out_hbm, heat_hbm, out, sems):
    rows, cols = part.shape
    pairs = [
        (heat_rim.at[:, pl.ds(0, BLOCK)], heat_hbm.at[:, pl.ds(0, BLOCK)]),
        (heat_in, heat_hbm.at[:, pl.ds(BLOCK, cols - 2 * BLOCK)]),
        (heat_rim.at[:, pl.ds(BLOCK, BLOCK)], heat_hbm.at[:, pl.ds(cols - BLOCK, BLOCK)]),
    ]
    copies = [pltpu.make_async_copy(a, b, sems.at[k]) for k, (a, b) in enumerate(pairs)]
    for copy in copies:
        copy.start()
    whole_near, whole_far = decode(near[...]), decode(far[...])
    for k, r0 in enumerate(range(0, rows, chunk)):
        r = pl.ds(r0, chunk)
        high, low = halo_parts(whole_near[r0 : r0 + chunk], whole_far[r0 : r0 + chunk])
        out[r] = part[r] + dot(high, halo[...]) + dot(low, halo[...])
        copy = pltpu.make_async_copy(out.at[r], out_hbm.at[r], sems.at[len(pairs) + k])
        copy.start()
        copies.append(copy)
    for copy in copies:
        copy.wait()


def heat_kernel(blocks, first_call, after, absorber, cosine, mass, absorption, flux, lit, *refs):
    if first_call:
        out, weights, beams, depth = refs
    else:
        weights, beams, out, depth = refs
    gases, levels, points = absorption.shape
    width = len(blocks) * BLOCK
    span = gases * levels
    any_lit = jnp.max(lit[...])

    @pl.when(any_lit == 0)
    def _():
        out[...] = jnp.zeros_like(out)

    @pl.when(any_lit > 0)
    def _():
        if first_call:
            table = absorption[...].astype(F32).reshape(span, points).T
            keep = iota((levels, span), 1) % levels <= iota((levels, span), 0)
            for g in range(points):
                row = jnp.where(keep, table[g : g + 1], 0.0).astype(BF16)
                weights[g * levels : (g + 1) * levels] = row
            column = jnp.broadcast_to(flux[...], (8, points)).T[:, :1]
            beams[...] = jnp.broadcast_to(column, beams.shape)
        amounts = jnp.concatenate([absorber[b * BLOCK : (b + 1) * BLOCK] for b in blocks], axis=0)
        cos = jnp.concatenate([cosine[:, b * BLOCK : (b + 1) * BLOCK] for b in blocks], axis=1)
        cos = cos.astype(F32)
        scale = jnp.broadcast_to(-math.log2(math.e) / cos, (8, width))
        depth[...] = dot(weights[...], amounts.T)
        strips = range(0, levels, 8)
        tiles = range(0, width, BLOCK)
        totals = {(r, t): jnp.zeros((8, BLOCK), F32) for r in strips for t in tiles}
        for g in range(points):
            beam = jnp.broadcast_to(beams[g : g + 1], (8, BLOCK))
            for r, t in totals:
                d = depth[g * levels + r : g * levels + r + 8, t : t + BLOCK]
                totals[r, t] += beam * jnp.exp2(d * scale[:, t : t + BLOCK])
        down = [jnp.concatenate([totals[r, t] for r in strips], axis=0) for t in tiles]
        down = jnp.concatenate(down, axis=1)
        top = jnp.sum(beams[...], axis=0, keepdims=True)
        top = jnp.concatenate([top] * len(blocks), axis=1)
        above = jnp.concatenate([top, down[:-1]], axis=0)
        value = cos * (above - down)
        lanes = iota(lit.shape, 1)
        for k, b in enumerate(blocks):
            tile = slice(k * BLOCK, (k + 1) * BLOCK)
            on = jnp.sum(jnp.where(lanes == b, lit[...], 0), axis=1, keepdims=True).astype(F32)
            weight = mass[:, b * BLOCK : (b + 1) * BLOCK].astype(F32)
            out[:, tile] = on * value[:, tile] / weight


def struct(shape, dtype=F32):
    return pltpu.VMEM(shape, dtype)


def shards(
    tracers, velocity, metric, absorber, cosine, mass, absorption, flux, lit, neighbour, edge
):
    count, levels, cols = tracers.shape
    gases, points, _ = absorption.shape
    peers = lax.axis_size("sfc")
    total = neighbour.shape[1] * peers
    rows = count * levels
    pair = [(i, i ^ 1) for i in range(peers)]
    cross = [(i, (i + 2 * (i % 2) - 1) % peers) for i in range(peers)]
    tr = tracers.reshape(rows, cols)
    vel = velocity.reshape(2 * levels, cols)
    metric = metric.reshape(1, cols)
    absorption = absorption.transpose(0, 2, 1)
    flux = flux.reshape(1, points)
    lit = lit.reshape(1, -1)
    side = struct((rows, BLOCK))
    packed = struct((rows // 2 + 8, BLOCK), jnp.int32)
    half = struct((rows, 2 * BLOCK), BF16)
    full = struct((rows, cols))

    def like(x):
        return struct(x.shape, x.dtype)

    moved = (tr, vel, metric, neighbour, edge, absorber, mass, absorption, flux, lit, cosine)
    sent, far, wide, fine, *moved = pl.pallas_call(
        functools.partial(rim_kernel, levels),
        in_specs=[HBM] * len(moved),
        out_specs=[VMEM] * (4 + len(moved)),
        out_shape=[packed, side, struct((2 * BLOCK, 2 * BLOCK), BF16), struct((BLOCK, 2 * BLOCK), BF16)]
        + [like(x) for x in moved],
        scratch_shapes=[pltpu.SemaphoreType.DMA((len(moved) + 4,))],
        compiler_params=params(),
        name="rims_first",
    )(*[pltpu.with_memory_space_constraint(x, pltpu.HBM) for x in moved])
    tr, vel, metric, neighbour, edge, absorber, mass, absorption, flux, lit, cosine = moved
    cosine = cosine.reshape(1, cols)
    from_far = lax.ppermute(sent, "sfc", cross)
    weights = struct((points * levels, gases * levels), BF16)
    beams = struct((points, BLOCK))

    def heat(after, blocks, name, *extra):
        out = struct((levels, len(blocks) * BLOCK))
        return pl.pallas_call(
            functools.partial(heat_kernel, blocks, not extra),
            in_specs=[HBM] + [VMEM] * (6 + len(extra)),
            out_specs=VMEM if extra else [VMEM] * 3,
            out_shape=out if extra else [out, weights, beams],
            scratch_shapes=[pltpu.VMEM((points * levels, len(blocks) * BLOCK), F32)],
            compiler_params=params(16),
            cost_estimate=cost(1e9),
            name=name,
        )(after, absorber, cosine, mass, absorption, flux, lit, *extra)

    sent, part, speed, local, halo = pl.pallas_call(
        functools.partial(first_kernel, total, levels),
        in_specs=[VMEM] * 8,
        out_specs=[VMEM] * 5,
        out_shape=[
            packed,
            full,
            struct((2 * levels, cols)),
            struct((cols, cols), BF16),
            struct((2 * BLOCK, cols), BF16),
        ],
        scratch_shapes=[pltpu.VMEM((rows, cols), BF16)] * 2,
        compiler_params=params(),
        cost_estimate=cost(1e9),
        name="first_local",
    )(tr, vel, metric, wide, fine, far, neighbour, edge)
    from_near = lax.ppermute(sent, "sfc", pair)
    heat_rim, weights, beams = heat(halo, (0, 3), "heat_rims")

    own_sent, own_far, high, low = pl.pallas_call(
        functools.partial(far2_kernel, levels),
        in_specs=[VMEM] * 9,
        out_specs=[VMEM] * 4,
        out_shape=[packed, side, half, half],
        compiler_params=params(),
        name="far_second",
    )(part, from_near, from_far, halo, wide, fine, tr, speed, heat_rim)
    next_far = lax.ppermute(own_sent, "sfc", cross)
    own_sent, own_near = pl.pallas_call(
        functools.partial(near2_kernel, levels),
        in_specs=[VMEM] * 9,
        out_specs=[VMEM] * 2,
        out_shape=[packed, side],
        compiler_params=params(),
        name="near_second",
    )(part, high, low, halo, wide, fine, tr, speed, heat_rim)
    next_near = lax.ppermute(own_sent, "sfc", pair)
    heat_in = heat(high, (1, 2), "heat_inner", weights, beams)
    part2 = pl.pallas_call(
        functools.partial(inner2_kernel, levels),
        in_specs=[VMEM] * 12,
        out_specs=VMEM,
        out_shape=full,
        scratch_shapes=[pltpu.VMEM((rows, cols), BF16)] * 2,
        compiler_params=params(),
        cost_estimate=cost(1e9),
        name="second_local",
    )(part, high, low, halo, local, wide, fine, tr, speed, heat_in, own_near, own_far)
    advanced, heating = pl.pallas_call(
        functools.partial(last_kernel, 2 * levels),
        in_specs=[VMEM] * 6,
        out_specs=[HBM] * 2,
        out_shape=[jax.ShapeDtypeStruct((rows, cols), F32), jax.ShapeDtypeStruct((levels, cols), F32)],
        scratch_shapes=[pltpu.VMEM((rows, cols), F32), pltpu.SemaphoreType.DMA((3 + count // 2,))],
        compiler_params=params(),
        name="last",
    )(part2, next_near, next_far, halo, heat_rim, heat_in)
    return advanced.reshape(tracers.shape), heating


def solution(mesh):
    placed = (
        P(None, None, ("grp", "sfc")),
        P(None, None, ("grp", "sfc")),
        P(("grp", "sfc")),
        P(("grp", "sfc"), None),
        P(("grp", "sfc")),
        P(None, ("grp", "sfc")),
        P(),
        P(),
        P(("grp", "sfc")),
        P(None, ("grp", "sfc")),
        P(None, ("grp", "sfc")),
    )
    return jax.shard_map(
        shards,
        mesh=mesh,
        in_specs=placed,
        out_specs=(P(None, None, ("grp", "sfc")), P(None, ("grp", "sfc"))),
        check_vma=False,
    )
```

```python
import functools
import math

import jax
import jax.numpy as jnp
import numpy as np
from jax import lax
from jax.experimental import pallas as pl
from jax.experimental.pallas import tpu as pltpu
from jax.sharding import PartitionSpec as P

BLOCK = 128
RIM = 8
STEP = 0.1
BITS = 21
LOWER = 32 - BITS
HALF = 1 << (BITS - 1)
SPAN = float(HALF - 8)
F32 = jnp.float32
BF16 = jnp.bfloat16
VMEM = pl.BlockSpec(memory_space=pltpu.VMEM)
SMEM = pl.BlockSpec(memory_space=pltpu.SMEM)
HBM = pl.BlockSpec(memory_space=pltpu.HBM)


def derivative_table():
    nodes = np.array([-1.0, -1.0 / math.sqrt(5.0), 1.0 / math.sqrt(5.0), 1.0])
    weights = np.array(
        [1.0 / np.prod([nodes[i] - nodes[m] for m in range(4) if m != i]) for i in range(4)]
    )
    table = np.zeros((4, 4))
    for i in range(4):
        for m in range(4):
            if i != m:
                table[i, m] = weights[m] / weights[i] / (nodes[i] - nodes[m])
        table[i, i] = -sum(table[i, m] for m in range(4) if m != i)
    return table


def params(mib=8):
    return pltpu.CompilerParams(vmem_limit_bytes=mib << 20)


def cost(flops, size=1 << 20):
    return pl.CostEstimate(flops=int(flops), bytes_accessed=int(size), transcendentals=0)


def iota(shape, dim):
    return lax.broadcasted_iota(jnp.int32, shape, dim)


def split(x):
    high = x.astype(BF16)
    return high, (x - high.astype(F32)).astype(BF16)


def dot(a, b):
    return jnp.dot(a, b, preferred_element_type=F32)


def build_derivatives(wide_ref, fine_ref):
    table = derivative_table()
    src, dst = iota((BLOCK, BLOCK), 0), iota((BLOCK, BLOCK), 1)
    si, sj, di, dj = src // 4 % 4, src % 4, dst // 4 % 4, dst % 4
    same = src // 16 == dst // 16
    halves = []
    for d, s, keep in ((di, si, same & (sj == dj)), (dj, sj, same & (si == di))):
        pick = jnp.where(keep, d * 4 + s, -1)
        value = jnp.zeros((BLOCK, BLOCK), F32)
        for i in range(4):
            for m in range(4):
                value = jnp.where(pick == i * 4 + m, float(table[i, m]), value)
        halves.append(value)
    high, low = split(jnp.concatenate(halves, axis=1))
    wide_ref[:BLOCK] = high
    wide_ref[BLOCK:] = high
    fine_ref[...] = low


def advance(field, first, second, wide_ref, fine_ref):
    high, low = split(field)
    both = dot(jnp.concatenate([high, low], axis=1), wide_ref[...]) + dot(high, fine_ref[...])
    return field + first * both[:, :BLOCK] + second * both[:, BLOCK:]


def repeat_rows(x, times):
    return jnp.concatenate([x] * times, axis=0) if times > 1 else x


def rim_starts(cols):
    near = jnp.where(lax.axis_index("sfc") % 2 == 0, cols - BLOCK, 0)
    return pl.multiple_of(near, BLOCK), pl.multiple_of(cols - BLOCK - near, BLOCK)


def rim_kernel(levels, *refs):
    count = (len(refs) - 5) // 2
    given, (sent, far, wide, fine), kept, sems = (
        refs[:count], refs[count : count + 4], refs[count + 4 : -1], refs[-1],
    )
    tr_hbm, vel_hbm, metric_hbm = given[:3]
    tr, vel, metric = kept[:3]
    rows, cols = tr.shape
    rims = [pl.ds(start, BLOCK) for start in rim_starts(cols)[::-1]]
    inner = pl.ds(BLOCK, cols - 2 * BLOCK)
    pairs = [(metric_hbm, metric)]
    pairs += [(hbm.at[:, r], ref.at[:, r]) for r in rims for hbm, ref in ((vel_hbm, vel), (tr_hbm, tr))]
    pairs += [(hbm.at[:, inner], ref.at[:, inner]) for hbm, ref in ((vel_hbm, vel), (tr_hbm, tr))]
    pairs += list(zip(given[3:], kept[3:], strict=True))
    copies = [pltpu.make_async_copy(a, b, sems.at[k]) for k, (a, b) in enumerate(pairs)]
    for copy in copies:
        copy.start()
    build_derivatives(wide, fine)
    copies[0].wait()
    for copy in copies[1:3]:
        copy.wait()
    rim = rims[0]
    scale = -STEP * metric[:, rim]
    first = repeat_rows(vel[:levels, rim] * scale, rows // levels)
    second = repeat_rows(vel[levels:, rim] * scale, rows // levels)
    field = advance(tr[:, rim], first, second, wide, fine)
    far[...] = field
    sent[...] = encode(field)
    for copy in copies[3:]:
        copy.wait()


def is_point(shape, *points):
    point = iota(shape, 1) % 16
    return functools.reduce(jnp.logical_or, [point == p for p in points])


def shifted(x, shift):
    return pltpu.roll(x, shift % BLOCK, 1)


def pack(rim):
    size = rim.shape[0] // 4
    a, b, c, d = (rim[k * size : (k + 1) * size] for k in range(4))
    shape = d.shape
    upper = is_point(shape, 5, 6)
    moved = (
        jnp.where(upper, shifted(d, 5), shifted(d, 7)),
        jnp.where(upper, shifted(d, -7), shifted(d, -5)),
        jnp.where(is_point(shape, 5, 9), shifted(d, 1), shifted(d, -1)),
    )
    inside = is_point(shape, 5, 6, 9, 10)
    return jnp.concatenate([jnp.where(inside, m, x) for m, x in zip(moved, (a, b, c), strict=True)], axis=0)


def encode(rim):
    packed = pack(rim)
    strips = [packed[r : r + 8] for r in range(0, packed.shape[0], 8)]
    largest = functools.reduce(jnp.maximum, [jnp.abs(x) for x in strips])
    power = jnp.clip(jnp.ceil(jnp.log2(largest) + 1e-3), -125.0, 125.0)
    scale = jnp.exp2(-power)
    count = len(strips) // 3
    words = [(x * scale * SPAN + (HALF + 0.5)).astype(jnp.int32) for x in strips]
    a, b, c = (words[k * count : (k + 1) * count] for k in range(3))
    first = [x | (z << BITS) for x, z in zip(a, c, strict=True)]
    second = [y | ((z >> LOWER) << BITS) for y, z in zip(b, c, strict=True)]
    return jnp.concatenate([power.astype(jnp.int32)] + first + second, axis=0)


def decode(sent):
    scale = jnp.exp2(sent[:8].astype(F32)) * (1.0 / SPAN)
    count = (sent.shape[0] - 8) // 16
    words = [sent[8 + r * 8 : 16 + r * 8] for r in range(2 * count)]
    a, b, c = [], [], []
    for first, second in zip(words[:count], words[count:], strict=True):
        a.append(first & (2 * HALF - 1))
        b.append(second & (2 * HALF - 1))
        upper = lax.shift_right_logical(second, BITS) << LOWER
        c.append(lax.shift_right_logical(first, BITS) | upper)
    return unpack(jnp.concatenate([(x - HALF).astype(F32) * scale for x in a + b + c], axis=0))


def unpack(sent):
    size = sent.shape[0] // 3
    a, b, c = (sent[k * size : (k + 1) * size] for k in range(3))
    shape = a.shape
    d = jnp.where(is_point(shape, 4, 8), shifted(c, -1), shifted(c, 1))
    d = jnp.where(is_point(shape, 0, 1), shifted(a, -5), d)
    d = jnp.where(is_point(shape, 2, 3), shifted(a, -7), d)
    d = jnp.where(is_point(shape, 12, 13), shifted(b, 7), d)
    d = jnp.where(is_point(shape, 14, 15), shifted(b, 5), d)
    return jnp.concatenate([a, b, c, d], axis=0)


def build_assembly(total, position, nb, ne, local, halo):
    elems, cols = nb.shape[1], local.shape[1]
    index = nb[...] - position * elems + RIM
    index = jnp.where(index < 0, index + total, index)
    index = jnp.where(index >= total, index - total, index)
    code = (index * 4 + ne[...]).astype(F32).astype(BF16)
    spread = (iota((elems, cols), 1) // 16 == iota((elems, cols), 0)).astype(F32).astype(BF16)
    code = dot(code, spread).astype(jnp.int32)
    lane = iota((1, cols), 1)
    i, j = lane // 4 % 4, lane % 4

    def source(code, p):
        edge, q = code % 4, 3 - p
        si = jnp.where(edge == 0, 0, jnp.where(edge == 1, q, jnp.where(edge == 2, 3, 3 - q)))
        sj = jnp.where(edge == 0, q, jnp.where(edge == 1, 3, jnp.where(edge == 2, 3 - q, 0)))
        return code // 4 * 16 + si * 4 + sj

    across = jnp.where(i == 0, source(code[0:1], j), source(code[2:3], 3 - j))
    across = jnp.where((i == 0) | (i == 3), across, -1)
    along = jnp.where(j == 3, source(code[1:2], i), source(code[3:4], 3 - i))
    along = jnp.where((j == 0) | (j == 3), along, -1)
    own = 1.0 - 0.5 * ((across >= 0).astype(F32) + (along >= 0).astype(F32))

    def rows_of(start):
        row = iota((BLOCK, cols), 0) + start
        return jnp.where(row == across, 0.5, 0.0) + jnp.where(row == along, 0.5, 0.0)

    even = position % 2 == 0
    halo[:BLOCK] = rows_of(jnp.where(even, BLOCK + cols, 0)).astype(BF16)
    halo[BLOCK:] = rows_of(jnp.where(even, 0, BLOCK + cols)).astype(BF16)
    for r in range(0, cols, BLOCK):
        value = rows_of(BLOCK + r) + jnp.where(iota((BLOCK, cols), 0) + r == lane, own, 0.0)
        local[r : r + BLOCK] = value.astype(BF16)


def first_kernel(
    total, levels, tr, vel, metric, wide, fine, far, nb, ne,
    sent, part, speed, local, halo, high, low,
):
    rows, cols = tr.shape
    scale = -STEP * metric[...]
    speed[...] = vel[...] * scale
    near_start, far_start = rim_starts(cols)
    for start in (near_start, *range(BLOCK, cols - BLOCK, BLOCK)):
        tile = pl.ds(start, BLOCK)
        first = repeat_rows(speed[:levels, tile], rows // levels)
        second = repeat_rows(speed[levels:, tile], rows // levels)
        field = advance(tr[:, tile], first, second, wide, fine)
        if start is near_start:
            sent[...] = encode(field)
        high[:, tile], low[:, tile] = split(field)
    tile = pl.ds(far_start, BLOCK)
    high[:, tile], low[:, tile] = split(far[...])
    build_assembly(total, lax.axis_index("sfc"), nb, ne, local, halo)
    part[...] = dot(high[...], local[...]) + dot(low[...], local[...])


def halo_parts(near, far):
    nh, nl = split(near)
    fh, fl = split(far)
    return jnp.concatenate([nh, fh], axis=1), jnp.concatenate([nl, fl], axis=1)


def second_rim(levels, start, part, high, low, halo, wide, fine, tr, speed, heat):
    rows, cols = part.shape
    tile = pl.ds(start, BLOCK)
    warm_tile = pl.ds(pl.multiple_of(jnp.where(start == 0, 0, BLOCK), BLOCK), BLOCK)
    section = part[:, tile] + dot(high[...], halo[:, tile]) + dot(low[...], halo[:, tile])
    first = repeat_rows(speed[:levels, tile], rows // levels)
    second = repeat_rows(speed[levels:, tile], rows // levels)
    field = 0.5 * (tr[:, tile] + advance(section, first, second, wide, fine))
    warm = (0.5 * STEP) * heat[:, warm_tile]
    return jnp.concatenate([field[:levels] + warm, field[levels:]], axis=0)


def far2_kernel(
    levels, part, near, sent, halo, wide, fine, tr, speed, heat, out_sent, out_far, high, low
):
    high[...], low[...] = halo_parts(decode(near[...]), decode(sent[...]))
    start = rim_starts(part.shape[1])[1]
    field = second_rim(levels, start, part, high, low, halo, wide, fine, tr, speed, heat)
    out_far[...] = field
    out_sent[...] = encode(field)


def near2_kernel(levels, part, high, low, halo, wide, fine, tr, speed, heat, sent, out):
    start = rim_starts(part.shape[1])[0]
    out[...] = second_rim(levels, start, part, high, low, halo, wide, fine, tr, speed, heat)
    sent[...] = encode(out[...])


def inner2_kernel(
    levels, part, high, low, halo, local, wide, fine, tr, speed, heat,
    own_near, own_far, out, own_high, own_low,
):
    rows, cols = part.shape
    inner = slice(BLOCK, cols - BLOCK)
    section = part[:, inner] + dot(high[...], halo[:, inner]) + dot(low[...], halo[:, inner])
    for b in range(BLOCK, cols - BLOCK, BLOCK):
        tile = slice(b, b + BLOCK)
        first = repeat_rows(speed[:levels, tile], rows // levels)
        second = repeat_rows(speed[levels:, tile], rows // levels)
        field = advance(section[:, b - BLOCK : b], first, second, wide, fine)
        field = 0.5 * (tr[:, tile] + field)
        warm = (0.5 * STEP) * heat[:, b - BLOCK : b]
        field = jnp.concatenate([field[:levels] + warm, field[levels:]], axis=0)
        own_high[:, tile], own_low[:, tile] = split(field)
    for start, value in zip(rim_starts(cols), (own_near, own_far), strict=True):
        tile = pl.ds(start, BLOCK)
        own_high[:, tile], own_low[:, tile] = split(value[...])
    out[...] = dot(own_high[...], local[...]) + dot(own_low[...], local[...])


def last_kernel(chunk, part, near, far, halo, heat_rim, heat_in, out_hbm, heat_hbm, out, sems):
    rows, cols = part.shape
    pairs = [
        (heat_rim.at[:, pl.ds(0, BLOCK)], heat_hbm.at[:, pl.ds(0, BLOCK)]),
        (heat_in, heat_hbm.at[:, pl.ds(BLOCK, cols - 2 * BLOCK)]),
        (heat_rim.at[:, pl.ds(BLOCK, BLOCK)], heat_hbm.at[:, pl.ds(cols - BLOCK, BLOCK)]),
    ]
    copies = [pltpu.make_async_copy(a, b, sems.at[k]) for k, (a, b) in enumerate(pairs)]
    for copy in copies:
        copy.start()
    whole_near, whole_far = decode(near[...]), decode(far[...])
    for k, r0 in enumerate(range(0, rows, chunk)):
        r = pl.ds(r0, chunk)
        high, low = halo_parts(whole_near[r0 : r0 + chunk], whole_far[r0 : r0 + chunk])
        out[r] = part[r] + dot(high, halo[...]) + dot(low, halo[...])
        copy = pltpu.make_async_copy(out.at[r], out_hbm.at[r], sems.at[len(pairs) + k])
        copy.start()
        copies.append(copy)
    for copy in copies:
        copy.wait()


def heat_kernel(blocks, first_call, after, absorber, cosine, mass, absorption, flux, lit, *refs):
    if first_call:
        out, weights, beams, depth = refs
    else:
        weights, beams, out, depth = refs
    gases, levels, points = absorption.shape
    width = len(blocks) * BLOCK
    span = gases * levels
    any_lit = jnp.max(lit[...])

    @pl.when(any_lit == 0)
    def _():
        out[...] = jnp.zeros_like(out)

    @pl.when(any_lit > 0)
    def _():
        if first_call:
            table = absorption[...].astype(F32).reshape(span, points).T
            keep = iota((levels, span), 1) % levels <= iota((levels, span), 0)
            for g in range(points):
                row = jnp.where(keep, table[g : g + 1], 0.0).astype(BF16)
                weights[g * levels : (g + 1) * levels] = row
            column = jnp.broadcast_to(flux[...], (8, points)).T[:, :1]
            beams[...] = jnp.broadcast_to(column, beams.shape)
        amounts = jnp.concatenate([absorber[b * BLOCK : (b + 1) * BLOCK] for b in blocks], axis=0)
        cos = jnp.concatenate([cosine[:, b * BLOCK : (b + 1) * BLOCK] for b in blocks], axis=1)
        cos = cos.astype(F32)
        scale = jnp.broadcast_to(-math.log2(math.e) / cos, (8, width))
        depth[...] = dot(weights[...], amounts.T)
        strips = range(0, levels, 8)
        tiles = range(0, width, BLOCK)
        totals = {(r, t): jnp.zeros((8, BLOCK), F32) for r in strips for t in tiles}
        for g in range(points):
            beam = jnp.broadcast_to(beams[g : g + 1], (8, BLOCK))
            for r, t in totals:
                d = depth[g * levels + r : g * levels + r + 8, t : t + BLOCK]
                totals[r, t] += beam * jnp.exp2(d * scale[:, t : t + BLOCK])
        down = [jnp.concatenate([totals[r, t] for r in strips], axis=0) for t in tiles]
        down = jnp.concatenate(down, axis=1)
        top = jnp.sum(beams[...], axis=0, keepdims=True)
        top = jnp.concatenate([top] * len(blocks), axis=1)
        above = jnp.concatenate([top, down[:-1]], axis=0)
        value = cos * (above - down)
        lanes = iota(lit.shape, 1)
        for k, b in enumerate(blocks):
            tile = slice(k * BLOCK, (k + 1) * BLOCK)
            on = jnp.sum(jnp.where(lanes == b, lit[...], 0), axis=1, keepdims=True).astype(F32)
            weight = mass[:, b * BLOCK : (b + 1) * BLOCK].astype(F32)
            out[:, tile] = on * value[:, tile] / weight


def struct(shape, dtype=F32):
    return pltpu.VMEM(shape, dtype)


def shards(
    tracers, velocity, metric, absorber, cosine, mass, absorption, flux, lit, neighbour, edge
):
    count, levels, cols = tracers.shape
    gases, points, _ = absorption.shape
    peers = lax.axis_size("sfc")
    total = neighbour.shape[1] * peers
    rows = count * levels
    pair = [(i, i ^ 1) for i in range(peers)]
    cross = [(i, (i + 2 * (i % 2) - 1) % peers) for i in range(peers)]
    tr = tracers.reshape(rows, cols)
    vel = velocity.reshape(2 * levels, cols)
    metric = metric.reshape(1, cols)
    absorption = absorption.transpose(0, 2, 1)
    flux = flux.reshape(1, points)
    lit = lit.reshape(1, -1)
    side = struct((rows, BLOCK))
    packed = struct((rows // 2 + 8, BLOCK), jnp.int32)
    half = struct((rows, 2 * BLOCK), BF16)
    full = struct((rows, cols))

    def like(x):
        return struct(x.shape, x.dtype)

    moved = (tr, vel, metric, neighbour, edge, absorber, mass, absorption, flux, lit, cosine)
    sent, far, wide, fine, *moved = pl.pallas_call(
        functools.partial(rim_kernel, levels),
        in_specs=[HBM] * len(moved),
        out_specs=[VMEM] * (4 + len(moved)),
        out_shape=[packed, side, struct((2 * BLOCK, 2 * BLOCK), BF16), struct((BLOCK, 2 * BLOCK), BF16)]
        + [like(x) for x in moved],
        scratch_shapes=[pltpu.SemaphoreType.DMA((len(moved) + 4,))],
        compiler_params=params(),
        name="rims_first",
    )(*[pltpu.with_memory_space_constraint(x, pltpu.HBM) for x in moved])
    tr, vel, metric, neighbour, edge, absorber, mass, absorption, flux, lit, cosine = moved
    cosine = cosine.reshape(1, cols)
    from_far = lax.ppermute(sent, "sfc", cross)
    weights = struct((points * levels, gases * levels), BF16)
    beams = struct((points, BLOCK))

    def heat(after, blocks, name, *extra):
        out = struct((levels, len(blocks) * BLOCK))
        return pl.pallas_call(
            functools.partial(heat_kernel, blocks, not extra),
            in_specs=[HBM] + [VMEM] * (6 + len(extra)),
            out_specs=VMEM if extra else [VMEM] * 3,
            out_shape=out if extra else [out, weights, beams],
            scratch_shapes=[pltpu.VMEM((points * levels, len(blocks) * BLOCK), F32)],
            compiler_params=params(16),
            cost_estimate=cost(1e9),
            name=name,
        )(after, absorber, cosine, mass, absorption, flux, lit, *extra)

    sent, part, speed, local, halo = pl.pallas_call(
        functools.partial(first_kernel, total, levels),
        in_specs=[VMEM] * 8,
        out_specs=[VMEM] * 5,
        out_shape=[
            packed,
            full,
            struct((2 * levels, cols)),
            struct((cols, cols), BF16),
            struct((2 * BLOCK, cols), BF16),
        ],
        scratch_shapes=[pltpu.VMEM((rows, cols), BF16)] * 2,
        compiler_params=params(),
        cost_estimate=cost(1e9),
        name="first_local",
    )(tr, vel, metric, wide, fine, far, neighbour, edge)
    from_near = lax.ppermute(sent, "sfc", pair)
    heat_rim, weights, beams = heat(halo, (0, 3), "heat_rims")

    own_sent, own_far, high, low = pl.pallas_call(
        functools.partial(far2_kernel, levels),
        in_specs=[VMEM] * 9,
        out_specs=[VMEM] * 4,
        out_shape=[packed, side, half, half],
        compiler_params=params(),
        name="far_second",
    )(part, from_near, from_far, halo, wide, fine, tr, speed, heat_rim)
    next_far = lax.ppermute(own_sent, "sfc", cross)
    own_sent, own_near = pl.pallas_call(
        functools.partial(near2_kernel, levels),
        in_specs=[VMEM] * 9,
        out_specs=[VMEM] * 2,
        out_shape=[packed, side],
        compiler_params=params(),
        name="near_second",
    )(part, high, low, halo, wide, fine, tr, speed, heat_rim)
    next_near = lax.ppermute(own_sent, "sfc", pair)
    heat_in = heat(high, (1, 2), "heat_inner", weights, beams)
    part2 = pl.pallas_call(
        functools.partial(inner2_kernel, levels),
        in_specs=[VMEM] * 12,
        out_specs=VMEM,
        out_shape=full,
        scratch_shapes=[pltpu.VMEM((rows, cols), BF16)] * 2,
        compiler_params=params(),
        cost_estimate=cost(1e9),
        name="second_local",
    )(part, high, low, halo, local, wide, fine, tr, speed, heat_in, own_near, own_far)
    advanced, heating = pl.pallas_call(
        functools.partial(last_kernel, 2 * levels),
        in_specs=[VMEM] * 6,
        out_specs=[HBM] * 2,
        out_shape=[jax.ShapeDtypeStruct((rows, cols), F32), jax.ShapeDtypeStruct((levels, cols), F32)],
        scratch_shapes=[pltpu.VMEM((rows, cols), F32), pltpu.SemaphoreType.DMA((3 + count // 2,))],
        compiler_params=params(),
        name="last",
    )(part2, next_near, next_far, halo, heat_rim, heat_in)
    return advanced.reshape(tracers.shape), heating


def solution(mesh):
    placed = (
        P(None, None, ("grp", "sfc")),
        P(None, None, ("grp", "sfc")),
        P(("grp", "sfc")),
        P(("grp", "sfc"), None),
        P(("grp", "sfc")),
        P(None, ("grp", "sfc")),
        P(),
        P(),
        P(("grp", "sfc")),
        P(None, ("grp", "sfc")),
        P(None, ("grp", "sfc")),
    )
    return jax.shard_map(
        shards,
        mesh=mesh,
        in_specs=placed,
        out_specs=(P(None, None, ("grp", "sfc")), P(None, ("grp", "sfc"))),
        check_vma=False,
    )
```
